32 devices in a mesh: section: 2 (over x), seq: 4 (over y, core), fsdp: 4 (over z).
Axes of the slice: x: 2, y: 2, z: 4, core: 2. Of those that a mesh axis runs over, the one named last changes fastest.
Arguments:
- boundary: bfloat16 [2, 24, 256, 768], P('section', 'fsdp', 'seq'), may hold values from -6 to 6
- timestep: int32 [24], P('fsdp'), may hold values from 0 to 999
- label: int32 [24], P('fsdp'), may hold values from 0 to 999
- label_table: bfloat16 [1000, 768], replicated, may hold values from -6 to 6
- ada_weight: bfloat16 [2, 768, 4608], P('section', 'fsdp'), may hold values from -0.21875 to 0.21875
- qkv_weight: bfloat16 [2, 768, 2304], P('section', 'fsdp'), may hold values from -0.21875 to 0.21875
- out_weight: bfloat16 [2, 768, 768], P('section', 'fsdp'), may hold values from -1.75 to 1.75
- up_weight: bfloat16 [2, 768, 3072], P('section', 'fsdp'), may hold values from -0.21875 to 0.21875
- down_weight: bfloat16 [2, 3072, 768], P('section', 'fsdp'), may hold values from -0.109375 to 0.109375
Outputs:
- end_rows: float32 [2, 24, 256, 768], P('section', 'fsdp', 'seq')
- cond_grad: float32 [2, 24, 768], P('section', 'fsdp')
- grad_ada: float32 [2, 768, 4608], P('section', 'fsdp', 'seq')
- grad_qkv: float32 [2, 768, 2304], P('section', 'fsdp')
- grad_out: float32 [2, 768, 768], P('section', 'fsdp')
- grad_up: float32 [2, 768, 3072], P('section', 'fsdp')
- grad_down: float32 [2, 3072, 768], P('section', 'fsdp')
The draws below stay inside these ranges and needn't reach their ends.
All inputs are finite; a program needn't handle non-finite values.
Results may differ from the reference program's by a relative error of at most 0.023.
Values may be sent and summed in bfloat16 or wider, within the bound.
No kernel may reach another device: no remote copies, remote signals or barrier semaphores. Data moves between devices by JAX's collectives and lax.ppermute only.
A program may use at most 256 MiB of HBM per device.

```python
import math
import jax
import jax.numpy as jnp
from jax import lax

D = 768
HEADS = 12
HD = 64
FF = 3072
CLASSES = 1000
TIMESTEPS = 1000
SEQ = 256
LATENTS = 24


def set_ends(entries, rng, smallest, top_value):
    spot = [jax.random.randint(jax.random.fold_in(rng, axis), (), 0, length) for axis, length in enumerate(entries.shape)]
    longest = entries.shape.index(max(entries.shape))
    neighbour = spot[:longest] + [(spot[longest] + 1) % entries.shape[longest]] + spot[longest + 1:]
    return entries.at[tuple(spot)].set(smallest).at[tuple(neighbour)].set(top_value)


def level_of(stream_key, shape, cuts, low, top_value):
    loudness = 1.0
    for position, parts in cuts:
        steps = jax.random.uniform(jax.random.fold_in(jax.random.fold_in(stream_key, 6), position), (parts,), jnp.float32, low / len(cuts), top_value / len(cuts))
        loudness = loudness * jnp.repeat(jnp.exp(steps), shape[position] // parts).reshape((-1,) + (1,) * (len(shape) - 1 - position))
    return loudness


def noise(stream_key, shape, width, most, pieces=(), held_as=jnp.bfloat16):
    result = width * jax.random.normal(stream_key, shape, jnp.float32)
    if pieces:
        result = result * level_of(stream_key, shape, pieces, -0.22, 0.18)
    return jnp.clip(result, -most, most).astype(held_as)


def setup_inputs(seed: int = 0) -> dict:
    streams_of = jax.random.split(jax.random.key(seed), 10)
    return {
        "boundary": noise(streams_of[0], (2, LATENTS, SEQ, D), 1.0, 6.0, ((0, 2), (1, 4), (2, 4))),
        "timestep": set_ends(jax.random.randint(streams_of[1], (LATENTS,), 0, TIMESTEPS), jax.random.fold_in(streams_of[1], 1), 0, TIMESTEPS - 1).astype(jnp.int32),
        "label": set_ends(jax.random.randint(streams_of[2], (LATENTS,), 0, CLASSES), jax.random.fold_in(streams_of[2], 1), 0, CLASSES - 1).astype(jnp.int32),
        "label_table": noise(streams_of[3], (CLASSES, D), 1.0, 6.0),
        "ada_weight": noise(streams_of[4], (2, D, 6 * D), D ** -0.5, 0.21875, ((0, 2), (1, 4))),
        "qkv_weight": noise(streams_of[5], (2, D, 3 * D), D ** -0.5, 0.21875, ((0, 2), (1, 4))),
        "out_weight": noise(streams_of[6], (2, D, D), (D // 64) ** -0.5, 1.75, ((0, 2), (1, 4))),
        "up_weight": noise(streams_of[7], (2, D, FF), D ** -0.5, 0.21875, ((0, 2), (1, 4))),
        "down_weight": noise(streams_of[8], (2, FF, D), FF ** -0.5, 0.109375, ((0, 2), (1, 4))),
    }


@jax.custom_vjp
def low(v):
    return lax.optimization_barrier(v.astype(jnp.bfloat16)).astype(jnp.float32)

@jax.custom_vjp
def low_back(v):
    return v

def low_keep(v):
    return (low(v), None)

def low_pass(kept, grad):
    return (grad,)

def back_keep(v):
    return (v, None)

def back_low(kept, grad):
    return (low(grad),)
low.defvjp(low_keep, low_pass)
low_back.defvjp(back_keep, back_low)
EPS = 1e-06
MAXIMAL_ACCURACY = lax.Precision.HIGHEST

def embed_time(timestep):
    half_width = D // 2
    frequency = jnp.exp(-math.log(10000.0) * jnp.arange(half_width, dtype=jnp.float32) / half_width)
    angles = timestep.astype(jnp.float32)[:, None] * frequency[None, :]
    return jnp.concatenate([jnp.cos(angles), jnp.sin(angles)], axis=1)

def normalize(array_in):
    centered = array_in - lax.optimization_barrier(jnp.mean(array_in, axis=-1, keepdims=True))
    return centered * lax.rsqrt(lax.optimization_barrier(jnp.mean(centered * centered, axis=-1, keepdims=True)) + EPS)

def transformer_layer(input_rows, condition_vector, adaptive_weight, query_key_value_weight, output_weight, up_matrix, down_matrix):
    latent_count, seq_len, model_width = input_rows.shape
    silu_cond = low(jax.nn.silu(condition_vector))
    modulation = low_back(jnp.dot(silu_cond, adaptive_weight, precision=MAXIMAL_ACCURACY))
    mod_parts = [modulation[:, None, part_no * model_width:(part_no + 1) * model_width] for part_no in range(6)]
    shift_one, scale_one, gate_one, shift_two, scale_two, gate_two = mod_parts
    attn_in = low(normalize(input_rows) * (1.0 + scale_one) + shift_one)
    qkv_rows = low(low_back(jnp.einsum('lsd,de->lse', attn_in, query_key_value_weight, precision=MAXIMAL_ACCURACY)))
    qkv_rows = qkv_rows.reshape(latent_count, seq_len, 3, HEADS, HD)
    queries = qkv_rows[:, :, 0]
    key_heads = qkv_rows[:, :, 1]
    value_heads = qkv_rows[:, :, 2]
    scores = low_back(jnp.einsum('lqhe,lkhe->lhqk', queries, key_heads, precision=MAXIMAL_ACCURACY) * (1.0 / math.sqrt(HD)))
    soft_weights = low(jax.nn.softmax(scores, axis=-1))
    attended = low(low_back(jnp.einsum('lhqk,lkhe->lqhe', soft_weights, value_heads, precision=MAXIMAL_ACCURACY)))
    attended = attended.reshape(latent_count, seq_len, model_width)
    projected = low_back(jnp.einsum('lsd,de->lse', attended, output_weight, precision=MAXIMAL_ACCURACY))
    midway = input_rows + gate_one * projected
    perceptron_input = low(normalize(midway) * (1.0 + scale_two) + shift_two)
    hidden_before = low_back(jnp.einsum('zwt,tj->zwj', perceptron_input, up_matrix, precision=MAXIMAL_ACCURACY))
    hidden_state = low(jax.nn.gelu(hidden_before, approximate=True))
    perceptron_output = low_back(jnp.einsum('eyq,qb->eyb', hidden_state, down_matrix, precision=MAXIMAL_ACCURACY))
    return midway + gate_two * perceptron_output

def two_layers(input_rows, condition_initial, condition_first, weight_collection):
    first_output = transformer_layer(input_rows, condition_initial, *(weight_matrix[0] for weight_matrix in weight_collection))
    passed_along = low(low_back(first_output))
    return transformer_layer(passed_along, condition_first, *(weight_matrix[1] for weight_matrix in weight_collection))

def reference(boundary, timestep, label, label_table, ada_weight, qkv_weight, out_weight, up_weight, down_weight):
    condition_vector = embed_time(timestep) + jnp.take(label_table, label, axis=0).astype(jnp.float32)
    weight_collection = tuple((weight_matrix.astype(jnp.float32) for weight_matrix in (ada_weight, qkv_weight, out_weight, up_weight, down_weight)))
    input_rows = boundary[0].astype(jnp.float32)
    cotangent = boundary[1].astype(jnp.float32)
    group_size = max((size_try for size_try in range(1, 17) if LATENTS % size_try == 0))
    block_count = LATENTS // group_size

    def scan_step(grad_total, block):
        block_in, block_cond, block_cot = block
        block_out, pullback = jax.vjp(two_layers, block_in, block_cond, block_cond, weight_collection)
        d_inputs, d_cond_zero, d_cond_one, d_weights = pullback(block_cot)
        grad_total = jax.tree.map(jnp.add, grad_total, d_weights)
        return (grad_total, (block_out, d_inputs, d_cond_zero, d_cond_one))
    zero_grads = tuple((jnp.zeros_like(weight_matrix) for weight_matrix in weight_collection))
    blocks = (input_rows.reshape(block_count, group_size, SEQ, D), condition_vector.reshape(block_count, group_size, D), cotangent.reshape(block_count, group_size, SEQ, D))
    grad_total, (outs_all, d_inputs, d_cond_zero, d_cond_one) = lax.scan(scan_step, zero_grads, blocks)
    end_rows = jnp.stack([d_inputs.reshape(LATENTS, SEQ, D), outs_all.reshape(LATENTS, SEQ, D)])
    cond_grad = jnp.stack([d_cond_zero.reshape(LATENTS, D), d_cond_one.reshape(LATENTS, D)])
    return (end_rows, cond_grad, grad_total[0], grad_total[1], grad_total[2], grad_total[3], grad_total[4])
```

```python
import math

import jax
import jax.numpy as jnp
from jax import lax
from jax.sharding import PartitionSpec as P

HD = 64
EPS = 1e-06
BF = jnp.bfloat16
F32 = jnp.float32


def dot(a, b, dims):
    return lax.dot_general(a, b, (dims, ((), ())), preferred_element_type=F32)


def mm(a, b):
    return dot(a, b, ((1,), (0,)))


def mm_nt(a, b):
    return dot(a, b, ((1,), (1,)))


def mm_tn(a, b):
    return dot(a, b, ((0,), (0,)))


def core_swap(x):
    return lax.ppermute(x, "seq", [(i, i ^ 1) for i in range(lax.axis_size("seq"))])


def y_swap(x):
    return lax.ppermute(x, "seq", [(i, i ^ 2) for i in range(lax.axis_size("seq"))])


def shift(x, axis, distance):
    n = lax.axis_size(axis)
    return lax.ppermute(x, axis, [(i, (i + distance) % n) for i in range(n)])


def roll_blocks(pieces, index):
    n = len(pieces)
    ordered = [pieces[(n - m) % n] for m in range(n)]
    doubled = jnp.stack(ordered + ordered[: n - 1])
    return lax.dynamic_slice_in_dim(doubled, (n - index) % n, n, 0)


def place_blocks(pieces, index):
    n = len(pieces)
    out = jnp.zeros((n,) + pieces[0].shape, pieces[0].dtype)
    for k in range(n):
        out = lax.dynamic_update_slice_in_dim(out, pieces[k][None], (index - k + n) % n, 0)
    return out


def small(n):
    return n <= 8


def gather_small(x, axis):
    n = lax.axis_size(axis)
    if not small(n):
        return lax.all_gather(x, axis)
    pieces = [x] + [shift(x, axis, k) for k in range(1, n)]
    return roll_blocks(pieces, lax.axis_index(axis))


def scatter_sum_small(x, axis):
    n = lax.axis_size(axis)
    if not small(n):
        return lax.psum_scatter(x, axis, scatter_dimension=0, tiled=False)
    me = lax.axis_index(axis)
    total = lax.dynamic_index_in_dim(x, me, 0, keepdims=False)
    for k in range(1, n):
        block = lax.dynamic_index_in_dim(x, (me + k) % n, 0, keepdims=False)
        total = total + shift(block, axis, k)
    return total


def exchange_small(x, axis):
    n = lax.axis_size(axis)
    if not small(n):
        return lax.all_to_all(x, axis, split_axis=0, concat_axis=0, tiled=True)
    me = lax.axis_index(axis)
    pieces = []
    for k in range(n):
        block = lax.dynamic_index_in_dim(x, (me + k) % n, 0, keepdims=False)
        pieces.append(block if k == 0 else shift(block, axis, k))
    return roll_blocks(pieces, me)


def ring_gather(mine, other):
    n = lax.axis_size("fsdp")
    if not small(n):
        whole = lax.all_gather(mine, "fsdp")
        return whole, y_swap(whole)
    me = lax.axis_index("fsdp")
    mine_pieces = [mine]
    other_pieces = [other]
    for _ in range(n - 1):
        mine_pieces.append(shift(mine_pieces[-1], "fsdp", 1))
        other_pieces.append(y_swap(mine_pieces[-1]))
    return place_blocks(mine_pieces, me), place_blocks(other_pieces, me)


def ring_scatter(blocks):
    n = lax.axis_size("fsdp")
    if not small(n):
        return lax.psum_scatter(blocks.astype(BF), "fsdp", scatter_dimension=0, tiled=False).astype(F32)
    me = lax.axis_index("fsdp")
    acc = lax.dynamic_index_in_dim(blocks, (me + n - 1) % n, 0, keepdims=False).astype(F32)
    for k in range(2, n + 1):
        arrived = shift(acc.astype(BF), "fsdp", 1)
        own = lax.dynamic_index_in_dim(blocks, (me + n - k) % n, 0, keepdims=False)
        acc = own.astype(F32) + arrived.astype(F32)
    return acc


def embed_time(timestep, width):
    half = width // 2
    frequency = jnp.exp(-math.log(10000.0) * jnp.arange(half, dtype=F32) / half)
    angles = timestep.astype(F32)[:, None] * frequency[None, :]
    return jnp.concatenate([jnp.cos(angles), jnp.sin(angles)], axis=1)


def normalize(v):
    centered = v - jnp.mean(v, axis=-1, keepdims=True)
    inv_std = lax.rsqrt(jnp.mean(centered * centered, axis=-1, keepdims=True) + EPS)
    return centered * inv_std, inv_std


def normalize_back(u, normed, inv_std):
    return inv_std * (
        u
        - jnp.mean(u, axis=-1, keepdims=True)
        - normed * jnp.mean(u * normed, axis=-1, keepdims=True)
    )


def gelu(v):
    return jax.nn.gelu(v, approximate=True)


def swap_sum(partial):
    own = partial.astype(BF)
    return own.astype(F32) + core_swap(own).astype(F32)


def forward(h, mods, w):
    wqkv, wout, wup, wdown, low = w
    latents, tokens, width = h.shape
    rows = latents * tokens
    shift_one, scale_one, gate_one, shift_two, scale_two, gate_two = mods
    normed_one, rstd_one = normalize(h)
    attn_in = (normed_one * (1.0 + scale_one) + shift_one).astype(BF)
    flat_in = attn_in.reshape(rows, width)
    qkv = [mm(flat_in, part).astype(BF) for part in wqkv]
    heads = wqkv[0].shape[1] // 3 // HD

    def pick(i):
        got = [p.reshape(latents, tokens, 3, heads, HD)[:, :, i] for p in qkv]
        return jnp.concatenate(got, axis=2)

    q, k, v = pick(0), pick(1), pick(2)
    scores = jnp.einsum("lqhe,lkhe->lhqk", q, k, preferred_element_type=F32) * (1.0 / math.sqrt(HD))
    probs32 = jax.nn.softmax(scores, axis=-1)
    probs = probs32.astype(BF)
    att = jnp.einsum("lhqk,lkhe->lqhe", probs, v, preferred_element_type=F32).astype(BF)
    att = att.reshape(rows, 2 * heads * HD)
    att_other = core_swap(att)
    att_first = jnp.where(low == 0, att, att_other)
    att_second = jnp.where(low == 0, att_other, att)
    attended = jnp.concatenate([att_first, att_second], axis=1)
    projected = mm(attended, wout).reshape(h.shape)
    midway = h + gate_one * projected
    normed_two, rstd_two = normalize(midway)
    mlp_in = (normed_two * (1.0 + scale_two) + shift_two).astype(BF)
    flat_mlp = mlp_in.reshape(rows, width)
    pre = [mm(flat_mlp, part) for part in wup]
    hidden = [gelu(p).astype(BF) for p in pre]
    partial = mm(hidden[0], wdown[0]) + mm(hidden[1], wdown[1])
    mlp_out = swap_sum(partial).reshape(h.shape)
    out = midway + gate_two * mlp_out
    saved = (normed_one, rstd_one, flat_in, q, k, v, probs32, attended, projected,
             normed_two, rstd_two, flat_mlp, pre, hidden, mlp_out)
    return out, saved


def backward(g, saved, mods, w):
    wqkv, wout, wup, wdown, low = w
    (normed_one, rstd_one, flat_in, q, k, v, probs32, attended, projected,
     normed_two, rstd_two, flat_mlp, pre, hidden, mlp_out) = saved
    latents, tokens, width = g.shape
    rows = latents * tokens
    shift_one, scale_one, gate_one, shift_two, scale_two, gate_two = mods
    d_mlp = (gate_two * g).astype(BF).reshape(rows, width)
    d_gate_two = jnp.sum(g * mlp_out, axis=1)
    d_pre = [
        jax.vjp(gelu, p)[1](mm_nt(d_mlp, part))[0].astype(BF) for p, part in zip(pre, wdown)
    ]
    partial = mm_nt(d_pre[0], wup[0]) + mm_nt(d_pre[1], wup[1])
    d_mlp_in = swap_sum(partial).reshape(g.shape)
    d_shift_two = jnp.sum(d_mlp_in, axis=1)
    d_scale_two = jnp.sum(d_mlp_in * normed_two, axis=1)
    d_midway = g + normalize_back(d_mlp_in * (1.0 + scale_two), normed_two, rstd_two)
    d_proj = (gate_one * d_midway).astype(BF).reshape(rows, width)
    d_gate_one = jnp.sum(d_midway * projected, axis=1)
    half = wout.shape[0] // 2
    own_out = lax.dynamic_slice_in_dim(wout, low * half, half, 0)
    d_att = mm_nt(d_proj, own_out).astype(BF)
    heads = half // HD
    d_heads = d_att.reshape(latents, tokens, heads, HD)
    scale = 1.0 / math.sqrt(HD)
    d_probs = jnp.einsum("lqhe,lkhe->lhqk", d_heads, v, preferred_element_type=F32)
    delta = jnp.sum(probs32 * d_probs, axis=-1, keepdims=True)
    d_scores = (probs32 * (d_probs - delta)).astype(BF)
    dq = (jnp.einsum("lhqk,lkhe->lqhe", d_scores, k, preferred_element_type=F32) * scale).astype(BF)
    dk = (jnp.einsum("lhqk,lqhe->lkhe", d_scores, q, preferred_element_type=F32) * scale).astype(BF)
    dv = jnp.einsum(
        "lhqk,lqhe->lkhe", probs32.astype(BF), d_heads, preferred_element_type=F32
    ).astype(BF)
    stacked = jnp.stack([dq, dk, dv], axis=2).reshape(latents, tokens, 3, 2, heads // 2 * HD)
    d_qkv = [stacked[:, :, :, i].reshape(rows, 3 * heads // 2 * HD) for i in range(2)]
    partial = mm_nt(d_qkv[0], wqkv[0]) + mm_nt(d_qkv[1], wqkv[1])
    d_attn_in = swap_sum(partial).reshape(g.shape)
    d_shift_one = jnp.sum(d_attn_in, axis=1)
    d_scale_one = jnp.sum(d_attn_in * normed_one, axis=1)
    d_h = d_midway + normalize_back(d_attn_in * (1.0 + scale_one), normed_one, rstd_one)
    d_mod = jnp.concatenate(
        [d_shift_one, d_scale_one, d_gate_one, d_shift_two, d_scale_two, d_gate_two], axis=1
    )
    return d_h, d_mod, d_mlp, d_pre, d_proj, d_qkv


def body(boundary, timestep, label, label_table, ada_weight, qkv_weight, out_weight, up_weight, down_weight):
    on_first = lax.axis_index("section") == 0
    seq = lax.axis_index("seq")
    low, high = seq % 2, seq // 2
    fsdp = lax.axis_index("fsdp")
    n_seq, n_fsdp = lax.axis_size("seq"), lax.axis_size("fsdp")
    assert n_seq == 4
    width = boundary.shape[-1]
    tokens_here = boundary.shape[2]
    latents = boundary.shape[1] // 2
    ada, wqkv, wout, wup, wdown = (a[0] for a in (ada_weight, qkv_weight, out_weight, up_weight, down_weight))
    share = wqkv.shape[0]

    own = boundary[0]
    stay = lax.dynamic_slice_in_dim(own, high * latents, latents, 0)
    leave = lax.dynamic_slice_in_dim(own, (1 - high) * latents, latents, 0)
    half = jnp.concatenate([stay, y_swap(leave)], axis=1)
    half_other = core_swap(half)
    rows_in = jnp.concatenate(
        [jnp.where(low == 0, half, half_other), jnp.where(low == 0, half_other, half)], axis=1
    )
    own_rows = rows_in.astype(F32)

    cond = embed_time(timestep, width) + jnp.take(label_table, label, axis=0).astype(F32)
    silu_cond = jax.nn.silu(cond).astype(BF)
    silu_all = gather_small(silu_cond, "fsdp").reshape(-1, width)
    silu_cols = lax.dynamic_slice_in_dim(silu_all, fsdp * share, share, 1)
    partial_mod = mm(silu_cols, ada).reshape(n_fsdp, 2, latents, ada.shape[1])
    partial_mod = lax.dynamic_index_in_dim(partial_mod, high, 1, keepdims=False)
    modulation = scatter_sum_small(partial_mod, "fsdp")
    mods = [modulation[:, None, p * width : (p + 1) * width] for p in range(6)]

    def quarters(a, axis):
        return (
            lax.dynamic_index_in_dim(a, 2 * low + high, axis, keepdims=False),
            lax.dynamic_index_in_dim(a, 2 * low + 1 - high, axis, keepdims=False),
        )

    sub = wdown.shape[0] // 4
    qkv_parts = [p.reshape(share, -1) for p in quarters(wqkv.reshape(share, 3, 4, width // 4), 2)]
    out_parts = quarters(wout.reshape(share, 4, width // 4), 1)
    up_parts = [p.reshape(share, -1) for p in quarters(wup.reshape(share, n_fsdp, 4, sub), 2)]
    down_parts = quarters(wdown.reshape(4, sub, width), 0)
    gathered_qkv = [g.reshape(width, -1) for g in ring_gather(*qkv_parts)]
    gathered_out = ring_gather(*out_parts)
    gathered_up = [g.reshape(width, -1) for g in ring_gather(*up_parts)]
    gathered_down = [g.reshape(-1, width) for g in ring_gather(*down_parts)]
    out_here = jnp.where(
        high == 0,
        jnp.concatenate([g.reshape(width, -1) for g in gathered_out], axis=1),
        jnp.concatenate([g.reshape(width, -1) for g in gathered_out[::-1]], axis=1),
    )
    out_there = core_swap(out_here)
    out_full = jnp.where(
        low == 0,
        jnp.concatenate([out_here, out_there], axis=1),
        jnp.concatenate([out_there, out_here], axis=1),
    )
    by_heads = out_full.reshape(2, 2, width // 4, width)
    by_heads = jnp.where(high == 0, by_heads, by_heads[:, ::-1])
    out_full = by_heads.reshape(width, width)
    weights = (gathered_qkv, out_full, gathered_up, gathered_down, low)

    first_out, _ = forward(own_rows, mods, weights)
    n_sec = lax.axis_size("section")

    def cross(x, step):
        rows = x.astype(BF)
        half_tokens = rows.shape[1] // 2
        mine = lax.dynamic_slice_in_dim(rows, low * half_tokens, half_tokens, 1)
        route = [(i, i + step) for i in range(n_sec) if 0 <= i + step < n_sec]
        here = lax.ppermute(mine, "section", route)
        there = core_swap(here)
        return jnp.concatenate(
            [jnp.where(low == 0, here, there), jnp.where(low == 0, there, here)], axis=1
        ).astype(F32)

    passed = cross(first_out, 1)
    layer_in = jnp.where(on_first, own_rows, passed)
    layer_out, saved = forward(layer_in, mods, weights)

    second_back = backward(own_rows, saved, mods, weights)
    incoming = cross(second_back[0], -1)
    grad = jnp.where(on_first, incoming, own_rows)
    d_h, d_mod, d_mlp, d_pre, d_proj, d_qkv = backward(grad, saved, mods, weights)
    flat_in, attended, flat_mlp, hidden = saved[2], saved[7], saved[11], saved[13]

    def y_first(mine, other):
        total = mine + y_swap(other.astype(BF)).astype(F32)
        return ring_scatter(total.reshape((n_fsdp, -1) + total.shape[1:]))

    def y_last(mine, other):
        both = jnp.concatenate([mine, other], axis=1)
        here = ring_scatter(both.reshape((n_fsdp, -1) + both.shape[1:])).astype(BF)
        there = y_swap(here).astype(F32)
        cut = here.shape[1] // 2
        return here.astype(F32) + jnp.concatenate([there[:, cut:], there[:, :cut]], axis=1)

    def spread(by_part):
        ordered = jnp.where(high == 0, by_part, by_part[::-1])
        other = core_swap(ordered)
        return jnp.concatenate(
            [jnp.where(low == 0, ordered, other), jnp.where(low == 0, other, ordered)], axis=0
        )

    def from_y_first(total):
        mine = total.astype(BF)
        return spread(jnp.stack([mine, y_swap(mine)]))

    def from_y_last(total):
        cut = total.shape[1] // 2
        return spread(jnp.stack([total[:, :cut], total[:, cut:]]).astype(BF))

    g_down = from_y_first(y_first(mm_tn(hidden[0], d_mlp), mm_tn(hidden[1], d_mlp)))
    g_down = g_down.reshape(wdown.shape).astype(F32)
    g_up = from_y_first(y_first(mm_tn(flat_mlp, d_pre[0]), mm_tn(flat_mlp, d_pre[1])))
    g_up = g_up.reshape(4, share, n_fsdp, sub).transpose(1, 2, 0, 3).reshape(wup.shape).astype(F32)
    quarter = width // 4
    out_cols = [
        lax.dynamic_slice_in_dim(d_proj, (2 * low + part) * quarter, quarter, 1)
        for part in (high, 1 - high)
    ]
    att_order = attended.reshape(-1, 2, 2, quarter)
    att_order = jnp.where(high == 0, att_order, att_order[:, :, ::-1]).reshape(-1, width)
    g_out = from_y_last(y_last(mm_tn(att_order, out_cols[0]), mm_tn(att_order, out_cols[1])))
    g_out = g_out.transpose(1, 0, 2).reshape(wout.shape).astype(F32)
    g_qkv = from_y_last(y_last(mm_tn(flat_in, d_qkv[0]), mm_tn(flat_in, d_qkv[1])))
    g_qkv = g_qkv.reshape(4, share, 3, quarter).transpose(1, 2, 0, 3).reshape(wqkv.shape).astype(F32)

    d_mine = d_mod.astype(BF)
    d_there = y_swap(d_mine)
    d_six = jnp.concatenate(
        [jnp.where(high == 0, d_mine, d_there), jnp.where(high == 0, d_there, d_mine)], axis=0
    )
    d_all = gather_small(d_six, "fsdp").reshape(-1, d_six.shape[1])
    ada_cols = ada.shape[1] // n_seq
    g_ada = mm_tn(silu_cols, lax.dynamic_slice_in_dim(d_all, seq * ada_cols, ada_cols, 1))
    d_silu = mm_nt(d_all, ada).reshape(n_fsdp, 2 * latents, share)
    d_silu = exchange_small(d_silu, "fsdp").transpose(1, 0, 2).reshape(2 * latents, width)
    cond_grad = jax.vjp(jax.nn.silu, cond)[1](d_silu)[0]

    result = jnp.where(on_first, d_h, layer_out)
    blocks = result.reshape(latents, 2, 2, tokens_here, width)
    blocks = lax.dynamic_index_in_dim(blocks, low, 1, keepdims=False)
    keep = blocks[:, 0]
    arrive = y_swap(blocks[:, 1].astype(BF)).astype(F32)
    end_rows = jnp.where(
        high == 0, jnp.concatenate([keep, arrive], axis=0), jnp.concatenate([arrive, keep], axis=0)
    )
    return (
        end_rows[None],
        cond_grad[None],
        g_ada[None],
        g_qkv[None],
        g_out[None],
        g_up[None],
        g_down[None],
    )


def solution(mesh):
    rows = P("section", "fsdp", "seq", None)
    weight = P("section", "fsdp", None)
    return jax.shard_map(
        body,
        mesh=mesh,
        in_specs=(rows, P("fsdp"), P("fsdp"), P(), weight, weight, weight, weight, weight),
        out_specs=(rows, weight, P("section", "fsdp", "seq"), weight, weight, weight, weight),
        check_vma=False,
    )
```

```python
import math

import jax
import jax.numpy as jnp
from jax import lax
from jax.experimental import pallas as pl
from jax.experimental.pallas import tpu as pltpu
from jax.sharding import PartitionSpec as P

HD = 64
EPS = 1e-06
BF = jnp.bfloat16
F32 = jnp.float32


def dot(a, b, dims):
    return lax.dot_general(a, b, (dims, ((), ())), preferred_element_type=F32)


def mm(a, b):
    return dot(a, b, ((1,), (0,)))


def mm_nt(a, b):
    return dot(a, b, ((1,), (1,)))


def mm_tn(a, b):
    return dot(a, b, ((0,), (0,)))


def core_swap(x):
    return lax.ppermute(x, "seq", [(i, i ^ 1) for i in range(lax.axis_size("seq"))])


def y_swap(x):
    return lax.ppermute(x, "seq", [(i, i ^ 2) for i in range(lax.axis_size("seq"))])


def shift(x, axis, distance):
    n = lax.axis_size(axis)
    return lax.ppermute(x, axis, [(i, (i + distance) % n) for i in range(n)])


def roll_blocks(pieces, index):
    n = len(pieces)
    ordered = [pieces[(n - m) % n] for m in range(n)]
    doubled = jnp.stack(ordered + ordered[: n - 1])
    return lax.dynamic_slice_in_dim(doubled, (n - index) % n, n, 0)


def place_blocks(pieces, index):
    n = len(pieces)
    out = jnp.zeros((n,) + pieces[0].shape, pieces[0].dtype)
    for k in range(n):
        out = lax.dynamic_update_slice_in_dim(out, pieces[k][None], (index - k + n) % n, 0)
    return out


def small(n):
    return n <= 8


def gather_small(x, axis):
    n = lax.axis_size(axis)
    if not small(n):
        return lax.all_gather(x, axis)
    pieces = [x] + [shift(x, axis, k) for k in range(1, n)]
    return roll_blocks(pieces, lax.axis_index(axis))


def scatter_sum_small(x, axis):
    n = lax.axis_size(axis)
    if not small(n):
        return lax.psum_scatter(x, axis, scatter_dimension=0, tiled=False)
    me = lax.axis_index(axis)
    total = lax.dynamic_index_in_dim(x, me, 0, keepdims=False)
    for k in range(1, n):
        block = lax.dynamic_index_in_dim(x, (me + k) % n, 0, keepdims=False)
        total = total + shift(block, axis, k)
    return total


def exchange_small(x, axis):
    n = lax.axis_size(axis)
    if not small(n):
        return lax.all_to_all(x, axis, split_axis=0, concat_axis=0, tiled=True)
    me = lax.axis_index(axis)
    pieces = []
    for k in range(n):
        block = lax.dynamic_index_in_dim(x, (me + k) % n, 0, keepdims=False)
        pieces.append(block if k == 0 else shift(block, axis, k))
    return roll_blocks(pieces, me)


ANY = pl.BlockSpec(memory_space=pl.ANY)
SCALARS = pl.BlockSpec(memory_space=pltpu.SMEM)
VMEM = pl.BlockSpec(memory_space=pltpu.VMEM)


def params(mib=48):
    return pltpu.CompilerParams(vmem_limit_bytes=mib << 20)


def cost(flops, moved):
    return pl.CostEstimate(flops=int(flops), bytes_accessed=int(moved), transcendentals=0)


def sized(shape, dtype):
    return jax.ShapeDtypeStruct(shape, dtype)


def pick_kernel(blocks, block, place, w_ref, *refs):
    own_ref, mine_ref = refs[-2:]
    for b in range(blocks):
        start = pl.multiple_of((2 * b + place[0]) * block, 128)
        own_ref[:, b * block : (b + 1) * block] = w_ref[:, pl.ds(start, block)]
    half = mine_ref.shape[0]
    mine_ref[...] = own_ref[pl.ds(pl.multiple_of(place[1] * half, 16), half), :]


def pick_columns(w, blocks, place, after=()):
    rows, cols = w.shape
    block = cols // blocks // 2
    half = rows // 2
    if block % 128 or half % 16:
        own = lax.dynamic_index_in_dim(w.reshape(rows, blocks, 2, block), place[0], 2, keepdims=False)
        own = own.reshape(rows, blocks * block)
        return own, lax.dynamic_slice_in_dim(own, place[1] * half, half, 0)
    return pl.pallas_call(
        lambda *refs: pick_kernel(blocks, block, *refs),
        out_shape=(sized((rows, cols // 2), w.dtype), sized((half, cols // 2), w.dtype)),
        in_specs=[SCALARS, VMEM] + [ANY] * len(after),
        out_specs=(VMEM, VMEM),
        compiler_params=params(),
        cost_estimate=cost(0, 2 * rows * cols * 2),
    )(place, w, *after)


def assemble_kernel(n, share, place, own_ref, *refs):
    mine_refs, other_refs, out_ref, sems = refs[: n - 1], refs[n - 1 : 2 * n - 2], refs[-2], refs[-1]
    half = share // 2
    me = place[2]

    def rows(start, size):
        return out_ref.at[pl.ds(pl.multiple_of(start, 16), size)]

    copies = [pltpu.make_async_copy(own_ref, rows(me * share, share), sems.at[0])]
    for k in range(1, n):
        base = lax.rem(me - k + n, n) * share
        for j, (ref, part) in enumerate(((mine_refs[k - 1], place[1]), (other_refs[k - 1], 1 - place[1]))):
            copies.append(
                pltpu.make_async_copy(ref, rows(base + part * half, half), sems.at[2 * k - 1 + j])
            )
    for copy in copies:
        copy.start()
    for copy in copies:
        copy.wait()


def assemble(own, mine, other, place):
    n = len(mine) + 1
    share = own.shape[0]
    return pl.pallas_call(
        lambda *refs: assemble_kernel(n, share, *refs),
        out_shape=sized((n * share, own.shape[1]), own.dtype),
        in_specs=[SCALARS] + [ANY] * (2 * n - 1),
        out_specs=ANY,
        scratch_shapes=[pltpu.SemaphoreType.DMA((2 * n - 1,))],
        compiler_params=params(),
        cost_estimate=cost(0, 2 * n * share * own.shape[1] * 2),
    )(place, own, *mine, *other)


def ring_step_list(mine):
    n = lax.axis_size("fsdp")
    arrived, there = [], []
    block = mine
    for _ in range(n - 1):
        block = shift(block, "fsdp", 1)
        arrived.append(block)
        there.append(y_swap(block))
    return arrived, there


def whole_weight(own, mine, place):
    n = lax.axis_size("fsdp")
    if not small(n):
        here = lax.all_gather(mine, "fsdp")
        there = y_swap(here)
        pair = jnp.where(place[1] == 0, jnp.stack([here, there], 1), jnp.stack([there, here], 1))
        return pair.reshape(n * own.shape[0], own.shape[1]), here
    arrived, there = ring_step_list(mine)
    return assemble(own, arrived, there, place), arrived[-1]


def ring_scatter(blocks):
    n = lax.axis_size("fsdp")
    if not small(n):
        return lax.psum_scatter(blocks.astype(BF), "fsdp", scatter_dimension=0, tiled=False).astype(F32)
    me = lax.axis_index("fsdp")
    acc = lax.dynamic_index_in_dim(blocks, (me + n - 1) % n, 0, keepdims=False).astype(F32)
    for k in range(2, n + 1):
        arrived = shift(acc.astype(BF), "fsdp", 1)
        own = lax.dynamic_index_in_dim(blocks, (me + n - k) % n, 0, keepdims=False)
        acc = own.astype(F32) + arrived.astype(F32)
    return acc


def embed_time(timestep, width):
    half = width // 2
    frequency = jnp.exp(-math.log(10000.0) * jnp.arange(half, dtype=F32) / half)
    angles = timestep.astype(F32)[:, None] * frequency[None, :]
    return jnp.concatenate([jnp.cos(angles), jnp.sin(angles)], axis=1)


def normalize(v):
    centered = v - jnp.mean(v, axis=-1, keepdims=True)
    inv_std = lax.rsqrt(jnp.mean(centered * centered, axis=-1, keepdims=True) + EPS)
    return centered * inv_std, inv_std


def normalize_back(u, normed, inv_std):
    return inv_std * (
        u
        - jnp.mean(u, axis=-1, keepdims=True)
        - normed * jnp.mean(u * normed, axis=-1, keepdims=True)
    )


ROOT = math.sqrt(2.0 / math.pi)


def gelu(v):
    return 0.5 * v * (1.0 + jnp.tanh(ROOT * (v + 0.044715 * (v * v * v))))


def gelu_slope(v):
    t = jnp.tanh(ROOT * (v + 0.044715 * (v * v * v)))
    inner = ROOT * (1.0 + 3.0 * 0.044715 * (v * v))
    return 0.5 * (1.0 + t) + 0.5 * v * (1.0 - t * t) * inner


def lanes_of(shape, which):
    lane = lax.broadcasted_iota(jnp.int32, shape, 1)
    return (lane < HD) if which == 0 else (lane >= HD)


def softmax_rows(s):
    e = jnp.exp(s - jnp.max(s, axis=-1, keepdims=True))
    return e / jnp.sum(e, axis=-1, keepdims=True)


def keep_head(pair, which):
    return jnp.where(lanes_of(pair.shape, which), pair, jnp.zeros_like(pair))


def attend_kernel(h_ref, mod_ref, w_ref, qkv_ref, att_ref, in_ref=None):
    h = h_ref[0].astype(F32)
    normed, _ = normalize(h)
    x = (normed * (1.0 + mod_ref[0, 1:2, :]) + mod_ref[0, 0:1, :]).astype(BF)
    if in_ref is not None:
        in_ref[0] = x
    cols = w_ref.shape[1] // 3
    for part in range(3):
        qkv_ref[0, :, part * cols : (part + 1) * cols] = mm(
            x, w_ref[:, part * cols : (part + 1) * cols]
        ).astype(BF)
    for pair in range(cols // (2 * HD)):
        at = pair * 2 * HD
        q = qkv_ref[0, :, at : at + 2 * HD]
        k = qkv_ref[0, :, cols + at : cols + at + 2 * HD]
        v = qkv_ref[0, :, 2 * cols + at : 2 * cols + at + 2 * HD]
        total = None
        for which in range(2):
            s = mm_nt(keep_head(q, which), k) * (1.0 / math.sqrt(HD))
            o = mm(softmax_rows(s).astype(BF), keep_head(v, which))
            total = o if total is None else total + o
        att_ref[0, :, at : at + 2 * HD] = total.astype(BF)


def row_spec(tokens, width):
    return pl.BlockSpec((1, tokens, width), lambda i: (i, 0, 0))


def mod_spec(parts, width):
    return pl.BlockSpec((1, parts, width), lambda i: (i, 0, 0))


def attend(h, mods, wqkv, keep):
    latents, tokens, width = h.shape
    cols = wqkv.shape[1]
    outs = [(cols, BF), (cols // 3, BF)] + ([(width, BF)] if keep else [])
    return pl.pallas_call(
        attend_kernel,
        grid=(latents,),
        out_shape=tuple(sized((latents, tokens, c), t) for c, t in outs),
        in_specs=[row_spec(tokens, width), mod_spec(6, width), VMEM],
        out_specs=tuple(row_spec(tokens, c) for c, _ in outs),
        compiler_params=params(),
        cost_estimate=cost(latents * tokens * (2 * width * cols + 8 * tokens * cols), 8 << 20),
    )(h, mods, wqkv)


CHUNK = 512


def mlp_kernel(place, h_ref, mod_ref, own_ref, other_ref, wout_ref, wup_ref, wdown_ref,
               part_ref, midway_ref, proj_ref=None, in_ref=None, pre_ref=None, hidden_ref=None):
    half = own_ref.shape[2]
    low = place[0]
    projected = mm(own_ref[0], wout_ref[pl.ds(pl.multiple_of(low * half, 128), half), :])
    projected += mm(other_ref[0], wout_ref[pl.ds(pl.multiple_of((1 - low) * half, 128), half), :])
    midway = h_ref[0].astype(F32) + mod_ref[0, 2:3, :] * projected
    midway_ref[0] = midway
    normed, _ = normalize(midway)
    x = (normed * (1.0 + mod_ref[0, 4:5, :]) + mod_ref[0, 3:4, :]).astype(BF)
    if proj_ref is not None:
        proj_ref[0] = projected.astype(BF)
        in_ref[0] = x
    total = None
    for at in range(0, wup_ref.shape[1], CHUNK):
        pre = mm(x, wup_ref[:, at : at + CHUNK])
        hidden = gelu(pre).astype(BF)
        if pre_ref is not None:
            pre_ref[0, :, at : at + CHUNK] = pre
            hidden_ref[0, :, at : at + CHUNK] = hidden
        part = mm(hidden, wdown_ref[at : at + CHUNK, :])
        total = part if total is None else total + part
    part_ref[0] = total.astype(BF)


def mlp(place, h, mods, own, other, wout, wup, wdown, keep):
    latents, tokens, width = h.shape
    units = wup.shape[1]
    half = own.shape[2]
    outs = [(width, BF), (width, F32)]
    if keep:
        outs += [(width, BF), (width, BF), (units, F32), (units, BF)]
    return pl.pallas_call(
        mlp_kernel,
        grid=(latents,),
        out_shape=tuple(sized((latents, tokens, c), t) for c, t in outs),
        in_specs=[SCALARS, row_spec(tokens, width), mod_spec(6, width), row_spec(tokens, half),
                  row_spec(tokens, half), VMEM, VMEM, VMEM],
        out_specs=tuple(row_spec(tokens, c) for c, _ in outs),
        compiler_params=params(),
        cost_estimate=cost(latents * tokens * 2 * width * (2 * units + width), 16 << 20),
    )(place, h, mods, own, other, wout, wup, wdown)


def mlp_back_kernel(g_ref, mod_ref, pre_ref, wdown_ref, wup_ref, part_ref, d_pre_ref):
    d_mlp = (mod_ref[0, 5:6, :] * g_ref[0].astype(F32)).astype(BF)
    total = None
    for at in range(0, wup_ref.shape[1], CHUNK):
        d_hidden = mm_nt(d_mlp, wdown_ref[at : at + CHUNK, :])
        d_pre = (d_hidden * gelu_slope(pre_ref[0, :, at : at + CHUNK])).astype(BF)
        d_pre_ref[0, :, at : at + CHUNK] = d_pre
        part = mm_nt(d_pre, wup_ref[:, at : at + CHUNK])
        total = part if total is None else total + part
    part_ref[0] = total.astype(BF)


def mlp_back(g, mods, pre, wdown, wup):
    latents, tokens, width = g.shape
    units = wup.shape[1]
    return pl.pallas_call(
        mlp_back_kernel,
        grid=(latents,),
        out_shape=(sized((latents, tokens, width), BF), sized((latents, tokens, units), BF)),
        in_specs=[row_spec(tokens, width), mod_spec(6, width), row_spec(tokens, units), VMEM, VMEM],
        out_specs=(row_spec(tokens, width), row_spec(tokens, units)),
        compiler_params=params(),
        cost_estimate=cost(latents * tokens * 4 * width * units, 14 << 20),
    )(g, mods, pre, wdown, wup)


def attend_back_kernel(place, own_ref, other_ref, g_ref, midway_ref, proj_ref, mod_ref, qkv_ref,
                       wout_ref, wqkv_ref, part_ref, d_mid_ref, d_proj_ref, d_qkv_ref, sums_ref):
    d_in = own_ref[0].astype(F32) + other_ref[0].astype(F32)
    normed, inv_std = normalize(midway_ref[0])
    sums_ref[0, 1:2, :] = jnp.sum(d_in, axis=0, keepdims=True)
    sums_ref[0, 2:3, :] = jnp.sum(d_in * normed, axis=0, keepdims=True)
    d_mid = g_ref[0].astype(F32) + normalize_back(d_in * (1.0 + mod_ref[0, 4:5, :]), normed, inv_std)
    d_mid_ref[0] = d_mid
    d_proj = (mod_ref[0, 2:3, :] * d_mid).astype(BF)
    d_proj_ref[0] = d_proj
    sums_ref[0, 0:1, :] = jnp.sum(d_mid * proj_ref[0].astype(F32), axis=0, keepdims=True)
    cols = wqkv_ref.shape[1] // 3
    low = place[0]
    d_att = mm_nt(d_proj, wout_ref[pl.ds(pl.multiple_of(low * cols, 128), cols), :]).astype(BF)
    scale = 1.0 / math.sqrt(HD)
    for pair in range(cols // (2 * HD)):
        at = pair * 2 * HD
        q = qkv_ref[0, :, at : at + 2 * HD]
        k = qkv_ref[0, :, cols + at : cols + at + 2 * HD]
        v = qkv_ref[0, :, 2 * cols + at : 2 * cols + at + 2 * HD]
        d_o = d_att[:, at : at + 2 * HD]
        dq = dk = dv = 0.0
        for which in range(2):
            q_one, d_one = keep_head(q, which), keep_head(d_o, which)
            probs = softmax_rows(mm_nt(q_one, k) * scale)
            d_probs = mm_nt(d_one, v)
            delta = jnp.sum(probs * d_probs, axis=-1, keepdims=True)
            d_s = (probs * (d_probs - delta)).astype(BF)
            dq += mm(d_s, keep_head(k, which))
            dk += mm_tn(d_s, q_one)
            dv += mm_tn(probs.astype(BF), d_one)
        d_qkv_ref[0, :, at : at + 2 * HD] = (dq * scale).astype(BF)
        d_qkv_ref[0, :, cols + at : cols + at + 2 * HD] = (dk * scale).astype(BF)
        d_qkv_ref[0, :, 2 * cols + at : 2 * cols + at + 2 * HD] = dv.astype(BF)
    part_ref[0] = mm_nt(d_qkv_ref[0], wqkv_ref[...]).astype(BF)


def attend_back(place, own, other, g, midway, projected, mods, qkv, wout, wqkv):
    latents, tokens, width = g.shape
    cols = wqkv.shape[1]
    rows = row_spec(tokens, width)
    return pl.pallas_call(
        attend_back_kernel,
        grid=(latents,),
        out_shape=(
            sized(g.shape, BF),
            sized(g.shape, F32),
            sized(g.shape, BF),
            sized((latents, tokens, cols), BF),
            sized((latents, 3, width), F32),
        ),
        in_specs=[SCALARS, rows, rows, rows, rows, rows, mod_spec(6, width), row_spec(tokens, cols), VMEM, VMEM],
        out_specs=(rows, rows, rows, row_spec(tokens, cols), mod_spec(3, width)),
        compiler_params=params(),
        cost_estimate=cost(latents * tokens * (2 * width * cols + 20 * tokens * cols), 14 << 20),
    )(place, own, other, g, midway, projected, mods, qkv, wout, wqkv)


def inputs_back_kernel(own_ref, other_ref, h_ref, d_mid_ref, mod_ref, d_h_ref, sums_ref):
    d_in = own_ref[0].astype(F32) + other_ref[0].astype(F32)
    normed, inv_std = normalize(h_ref[0].astype(F32))
    sums_ref[0, 0:1, :] = jnp.sum(d_in, axis=0, keepdims=True)
    sums_ref[0, 1:2, :] = jnp.sum(d_in * normed, axis=0, keepdims=True)
    d_h = d_mid_ref[0] + normalize_back(d_in * (1.0 + mod_ref[0, 1:2, :]), normed, inv_std)
    d_h_ref[0] = d_h.astype(d_h_ref.dtype)


def inputs_back(own, other, h, d_mid, mods, dtype):
    latents, tokens, width = h.shape
    rows = row_spec(tokens, width)
    return pl.pallas_call(
        inputs_back_kernel,
        grid=(latents,),
        out_shape=(sized(h.shape, dtype), sized((latents, 2, width), F32)),
        in_specs=[rows, rows, rows, rows, mod_spec(6, width)],
        out_specs=(rows, mod_spec(2, width)),
        compiler_params=params(),
        cost_estimate=cost(0, 10 << 20),
    )(own, other, h, d_mid, mods)


def body(boundary, timestep, label, label_table, ada_weight, qkv_weight, out_weight, up_weight, down_weight):
    on_first = lax.axis_index("section") == 0
    seq = lax.axis_index("seq")
    low, high = seq % 2, seq // 2
    fsdp = lax.axis_index("fsdp")
    n_seq, n_fsdp, n_sec = lax.axis_size("seq"), lax.axis_size("fsdp"), lax.axis_size("section")
    assert n_seq == 4
    place = jnp.stack([low, high, fsdp]).astype(jnp.int32)
    width = boundary.shape[-1]
    tokens_here = boundary.shape[2]
    latents = boundary.shape[1] // 2
    ada, wqkv, wout, wup, wdown = (a[0] for a in (ada_weight, qkv_weight, out_weight, up_weight, down_weight))
    share = wqkv.shape[0]

    def by_core(here, there):
        return jnp.where(low == 0, here, there), jnp.where(low == 0, there, here)

    qkv_own, qkv_mine = pick_columns(wqkv, 3, place)
    full_qkv, token = whole_weight(qkv_own, qkv_mine, place)

    own = boundary[0]
    stay = lax.dynamic_slice_in_dim(own, high * latents, latents, 0)
    leave = lax.dynamic_slice_in_dim(own, (1 - high) * latents, latents, 0)
    half = jnp.concatenate([stay, y_swap(leave)], axis=1)
    own_rows = jnp.concatenate(by_core(half, core_swap(half)), axis=1)

    cond = embed_time(timestep, width) + jnp.take(label_table, label, axis=0).astype(F32)
    silu_cond = jax.nn.silu(cond).astype(BF)
    silu_all = gather_small(silu_cond, "fsdp").reshape(-1, width)
    silu_cols = lax.dynamic_slice_in_dim(silu_all, fsdp * share, share, 1)
    partial_mod = mm(silu_cols, ada).reshape(n_fsdp, 2, latents, ada.shape[1])
    partial_mod = lax.dynamic_index_in_dim(partial_mod, high, 1, keepdims=False)
    modulation = scatter_sum_small(partial_mod, "fsdp")
    mods = modulation.reshape(latents, 6, width)

    quarter = share // 4
    out_own = lax.dynamic_slice_in_dim(wout, (2 * high + low) * quarter, quarter, 0)
    if small(n_fsdp):
        out_arrived, out_there = ring_step_list(out_own)
        out_two = jnp.stack([jnp.stack(out_arrived), jnp.stack(out_there)], 1)
        out_two = jnp.where(high == 0, out_two, out_two[:, ::-1])
        out_four = jnp.stack(by_core(out_two, core_swap(out_two)), 2)
        pieces = [wout] + [out_four[k].reshape(share, width) for k in range(n_fsdp - 1)]
        full_out = place_blocks(pieces, fsdp).reshape(-1, width)
    else:
        full_out = lax.all_gather(wout, "fsdp", axis=0, tiled=True)
    up_own, up_mine = pick_columns(wup, n_fsdp, place, (token,))
    full_up, _ = whole_weight(up_own, up_mine, place)
    sub = wdown.shape[0] // 2
    down_own = lax.dynamic_slice_in_dim(wdown, low * sub, sub, 0)
    down_mine = lax.dynamic_slice_in_dim(down_own, high * (sub // 2), sub // 2, 0)
    full_down, _ = whole_weight(down_own, down_mine, place)

    def cross(rows, step):
        half_tokens = rows.shape[1] // 2
        mine = lax.dynamic_slice_in_dim(rows, low * half_tokens, half_tokens, 1)
        route = [(i, i + step) for i in range(n_sec) if 0 <= i + step < n_sec]
        here = lax.ppermute(mine, "section", route)
        return jnp.concatenate(by_core(here, core_swap(here)), axis=1)

    gate_two = mods[:, 5:6]

    _, att = attend(own_rows, mods, full_qkv, False)
    part, midway = mlp(place, own_rows, mods, att, core_swap(att), full_out, full_up, full_down, False)
    mlp_out = part.astype(F32) + core_swap(part).astype(F32)
    passed = cross((midway + gate_two * mlp_out).astype(BF), 1)

    h = jnp.where(on_first, own_rows, passed)
    qkv, att, attn_in = attend(h, mods, full_qkv, True)
    att_other = core_swap(att)
    part, midway, projected, mlp_in, pre, hidden = mlp(
        place, h, mods, att, att_other, full_out, full_up, full_down, True
    )
    mlp_out = part.astype(F32) + core_swap(part).astype(F32)
    layer_out = midway + gate_two * mlp_out

    def backward(g, dtype):
        part, d_pre = mlp_back(g, mods, pre, full_down, full_up)
        part_two, d_mid, d_proj, d_qkv, sums_mid = attend_back(
            place, part, core_swap(part), g, midway, projected, mods, qkv, full_out, full_qkv
        )
        d_h, sums_in = inputs_back(part_two, core_swap(part_two), h, d_mid, mods, dtype)
        return d_h, d_pre, d_proj, d_qkv, sums_mid, sums_in

    incoming = cross(backward(own_rows, BF)[0], -1)
    g = jnp.where(on_first, incoming, own_rows)
    d_mlp = (gate_two * g.astype(F32)).astype(BF)
    d_gate_two = jnp.sum(g.astype(F32) * mlp_out, axis=1)
    d_h, d_pre, d_proj, d_qkv, sums_mid, sums_in = backward(g, F32)

    def flat(a):
        return a.reshape(-1, a.shape[-1])

    def halves(a):
        split = a.reshape(n_fsdp, 2, -1, a.shape[-1])
        return (
            lax.dynamic_index_in_dim(split, high, 1, keepdims=False),
            lax.dynamic_index_in_dim(split, 1 - high, 1, keepdims=False),
        )

    def y_first(a):
        mine, other = halves(a)
        total = ring_scatter(mine.astype(F32) + y_swap(other.astype(BF)).astype(F32)).astype(BF)
        there = y_swap(total)
        return jnp.where(
            high == 0, jnp.concatenate([total, there]), jnp.concatenate([there, total])
        )

    def y_last(a):
        here = ring_scatter(a.reshape(n_fsdp, -1, a.shape[-1])).astype(BF)
        return (here.astype(F32) + y_swap(here).astype(F32)).astype(BF)

    def both_cores(a, blocks):
        rows = a.shape[0]
        pair = [p.reshape(rows, blocks, -1) for p in by_core(a, core_swap(a))]
        return jnp.stack(pair, 2).reshape(rows, -1).astype(F32)

    g_down = y_first(mm_tn(flat(hidden), flat(d_mlp)))
    g_down = jnp.concatenate(by_core(g_down, core_swap(g_down))).astype(F32)
    g_up = both_cores(y_first(mm_tn(flat(mlp_in), flat(d_pre))), n_fsdp)
    cols = width // 2
    own_cols = lax.dynamic_slice_in_dim(flat(d_proj), low * cols, cols, 1)
    attended = jnp.concatenate(by_core(flat(att), flat(att_other)), axis=1)
    g_out = both_cores(y_last(mm_tn(attended, own_cols)), 1)
    g_qkv = both_cores(y_last(mm_tn(flat(attn_in), flat(d_qkv))), 3)

    d_mod = jnp.concatenate([flat_sums.reshape(latents, -1) for flat_sums in (sums_in, sums_mid, d_gate_two)], axis=1)
    d_mine = d_mod.astype(BF)
    d_there = y_swap(d_mine)
    d_six = jnp.where(
        high == 0, jnp.concatenate([d_mine, d_there]), jnp.concatenate([d_there, d_mine])
    )
    d_all = gather_small(d_six, "fsdp").reshape(-1, d_six.shape[1])
    ada_cols = ada.shape[1] // n_seq
    g_ada = mm_tn(silu_cols, lax.dynamic_slice_in_dim(d_all, seq * ada_cols, ada_cols, 1))
    d_silu = mm_nt(d_all, ada).reshape(n_fsdp, 2 * latents, share)
    d_silu = exchange_small(d_silu, "fsdp").transpose(1, 0, 2).reshape(2 * latents, width)
    cond_grad = jax.vjp(jax.nn.silu, cond)[1](d_silu)[0]

    result = jnp.where(on_first, d_h, layer_out)
    blocks = result.reshape(latents, 2, 2, tokens_here, width)
    blocks = lax.dynamic_index_in_dim(blocks, low, 1, keepdims=False)
    keep = blocks[:, 0]
    arrive = y_swap(blocks[:, 1].astype(BF)).astype(F32)
    end_rows = jnp.where(
        high == 0, jnp.concatenate([keep, arrive], axis=0), jnp.concatenate([arrive, keep], axis=0)
    )
    return (
        end_rows[None],
        cond_grad[None],
        g_ada[None],
        g_qkv[None],
        g_out[None],
        g_up[None],
        g_down[None],
    )


def solution(mesh):
    rows = P("section", "fsdp", "seq", None)
    weight = P("section", "fsdp", None)
    return jax.shard_map(
        body,
        mesh=mesh,
        in_specs=(rows, P("fsdp"), P("fsdp"), P(), weight, weight, weight, weight, weight),
        out_specs=(rows, weight, P("section", "fsdp", "seq"), weight, weight, weight, weight),
        check_vma=False,
    )
```

```python
import math

import jax
import jax.numpy as jnp
from jax import lax
from jax.experimental import pallas as pl
from jax.experimental.pallas import tpu as pltpu
from jax.sharding import PartitionSpec as P

HD = 64
EPS = 1e-06
BF = jnp.bfloat16
F32 = jnp.float32


def dot(a, b, dims):
    return lax.dot_general(a, b, (dims, ((), ())), preferred_element_type=F32)


def mm(a, b):
    return dot(a, b, ((1,), (0,)))


def mm_nt(a, b):
    return dot(a, b, ((1,), (1,)))


def mm_tn(a, b):
    return dot(a, b, ((0,), (0,)))


def after(x, *tokens):
    return lax.optimization_barrier((x,) + tokens)[0]


def core_swap(x):
    return lax.ppermute(x, "seq", [(i, i ^ 1) for i in range(lax.axis_size("seq"))])


def y_swap(x):
    return lax.ppermute(x, "seq", [(i, i ^ 2) for i in range(lax.axis_size("seq"))])


def shift(x, axis, distance):
    n = lax.axis_size(axis)
    return lax.ppermute(x, axis, [(i, (i + distance) % n) for i in range(n)])


def small(n):
    return n == 4


def gather_back(x, axis):
    n = lax.axis_size(axis)
    if not small(n):
        whole = jnp.flip(lax.all_gather(x, axis), 0)
        doubled = jnp.concatenate([whole, whole])
        whole = lax.dynamic_slice_in_dim(doubled, n - 1 - lax.axis_index(axis), n, 0)
        return [whole[k] for k in range(n)]
    return [x] + [shift(x, axis, k) for k in range(1, n)]


def send_back(x, axis):
    n = lax.axis_size(axis)
    if not small(n):
        me = lax.axis_index(axis)
        doubled = jnp.concatenate([x, x])
        whole = jnp.flip(lax.dynamic_slice_in_dim(doubled, (me + 1) % n, n, 0), 0)
        got = lax.all_to_all(whole, axis, split_axis=0, concat_axis=0, tiled=True)
        got = lax.dynamic_slice_in_dim(jnp.concatenate([got, got]), me, n, 0)
        return [got[k] for k in range(n)]
    return [x[0]] + [shift(x[k], axis, n - k) for k in range(1, n)]


def together(pieces, token):
    return jnp.stack(lax.optimization_barrier(tuple(pieces) + (token,))[:-1])


ANY = pl.BlockSpec(memory_space=pl.ANY)
SCALARS = pl.BlockSpec(memory_space=pltpu.SMEM)
VMEM = pl.BlockSpec(memory_space=pltpu.VMEM)


def params(mib=48):
    return pltpu.CompilerParams(vmem_limit_bytes=mib << 20)


def cost(flops, moved):
    return pl.CostEstimate(flops=int(flops), bytes_accessed=int(moved), transcendentals=0)


def sized(shape, dtype):
    return jax.ShapeDtypeStruct(shape, dtype)


def pick_kernel(blocks, place, *refs):
    w_refs, (own_ref, mine_ref) = refs[:-2], refs[-2:]
    at = 0
    for w_ref, count in zip(w_refs, blocks):
        block = w_ref.shape[1] // count // 2
        for b in range(count):
            start = pl.multiple_of((2 * b + place[0]) * block, 128)
            own_ref[:, at : at + block] = w_ref[:, pl.ds(start, block)]
            at += block
    half = mine_ref.shape[0]
    mine_ref[...] = own_ref[pl.ds(pl.multiple_of(place[1] * half, 16), half), :]


def pick_columns(ws, blocks, place):
    rows = ws[0].shape[0]
    half = rows // 2
    sizes = [w.shape[1] // count // 2 for w, count in zip(ws, blocks)]
    if half % 16 or any(size % 128 for size in sizes):
        own = jnp.concatenate(
            [
                lax.dynamic_index_in_dim(w.reshape(rows, count, 2, -1), place[0], 2, keepdims=False).reshape(rows, -1)
                for w, count in zip(ws, blocks)
            ],
            axis=1,
        )
        return own, lax.dynamic_slice_in_dim(own, place[1] * half, half, 0)
    cols = sum(w.shape[1] for w in ws) // 2
    return pl.pallas_call(
        lambda *refs: pick_kernel(blocks, *refs),
        out_shape=(sized((rows, cols), BF), sized((half, cols), BF)),
        in_specs=[SCALARS] + [VMEM] * len(ws),
        out_specs=(VMEM, VMEM),
        compiler_params=params(),
        cost_estimate=cost(0, 8 * rows * cols),
    )(place, *ws)


def assemble_kernel(n, share, place, own_ref, *refs):
    mine_refs, other_refs, out_ref, sems = refs[: n - 1], refs[n - 1 : 2 * n - 2], refs[-2], refs[-1]
    half = share // 2
    me = place[2]

    def rows(start, size):
        return out_ref.at[pl.ds(pl.multiple_of(start, 16), size)]

    copies = [pltpu.make_async_copy(own_ref, rows(me * share, share), sems.at[0])]
    for k in range(1, n):
        base = lax.rem(me - k + n, n) * share
        for j, (ref, part) in enumerate(((mine_refs[k - 1], place[1]), (other_refs[k - 1], 1 - place[1]))):
            copies.append(
                pltpu.make_async_copy(ref, rows(base + part * half, half), sems.at[2 * k - 1 + j])
            )
    for copy in copies:
        copy.start()
    for copy in copies:
        copy.wait()


def assemble(own, mine, other, place):
    n = len(mine) + 1
    share = own.shape[0]
    return pl.pallas_call(
        lambda *refs: assemble_kernel(n, share, *refs),
        out_shape=sized((n * share, own.shape[1]), own.dtype),
        in_specs=[SCALARS] + [ANY] * (2 * n - 1),
        out_specs=ANY,
        scratch_shapes=[pltpu.SemaphoreType.DMA((2 * n - 1,))],
        compiler_params=params(),
        cost_estimate=cost(0, 2 * n * share * own.shape[1] * 2),
    )(place, own, *mine, *other)


def whole_weights(owns, mines, place, between):
    n = lax.axis_size("fsdp")
    if not small(n):
        between(1, 0, mines[0])
        between(2, 2, mines[0])
        whole = []
        for own, mine in zip(owns, mines):
            here = lax.all_gather(mine, "fsdp")
            there = y_swap(here)
            pair = jnp.where(place[1] == 0, jnp.stack([here, there], 1), jnp.stack([there, here], 1))
            whole.append(pair.reshape(n * own.shape[0], own.shape[1]))
        return whole
    runs = [shift(mine, "fsdp", 1) for mine in mines]
    arrived, there = [[] for _ in mines], [[] for _ in mines]
    last, swaps = mines[0], []
    for k in range(1, n):
        for i in range(len(runs)):
            block = after(runs[i], last, *swaps[-2:-1])
            arrived[i].append(block)
            if k < n - 1:
                runs[i] = shift(block, "fsdp", 1)
            swaps.append(y_swap(block))
            there[i].append(swaps[-1])
            last = between(k, i, block)
    return [assemble(*four, place) for four in zip(owns, arrived, there)]


def join_kernel(place, here_ref, there_ref, out_ref):
    cols = there_ref.shape[1]
    here = here_ref[:, here_ref.shape[1] - cols :]
    out_ref[:, pl.ds(pl.multiple_of(place[0] * cols, 128), cols)] = here
    out_ref[:, pl.ds(pl.multiple_of((1 - place[0]) * cols, 128), cols)] = there_ref[...]


def join_cores(here, cols, place):
    rows = here.shape[0]
    there = core_swap(here[:, here.shape[1] - cols :])
    return pl.pallas_call(
        join_kernel,
        out_shape=sized((rows, 2 * cols), here.dtype),
        in_specs=[SCALARS, VMEM, VMEM],
        out_specs=VMEM,
        compiler_params=params(),
        cost_estimate=cost(0, 8 * rows * cols),
    )(place, here, there)


def ring_block(blocks, back):
    n = lax.axis_size("fsdp")
    return lax.dynamic_index_in_dim(blocks, (lax.axis_index("fsdp") + n - back) % n, 0, keepdims=False)


def ring_add(blocks, back, arrived):
    return (ring_block(blocks, back).astype(F32) + arrived.astype(F32)).astype(BF)


def grad_kernel(group, split, place, x_ref, d_ref, *refs):
    out_refs, whole_ref = refs[:-1], refs[-1]
    whole_ref[...] = mm_tn(x_ref[...], d_ref[...])
    size = out_refs[0].shape[1]
    for z in range(out_refs[0].shape[0]):
        for ref, part in zip(out_refs, (place[1], 1 - place[1]) if split else (0,)):
            start = pl.multiple_of(z * group + part * size, 8)
            ref[z] = whole_ref[pl.ds(start, size), :].astype(BF)


def weight_grad(x, d, place, split):
    n = lax.axis_size("fsdp")
    rows, cols = x.shape
    out = d.shape[1]
    group = cols // n
    block = min(cols, 384)
    if group > block or block % group or cols % block or group % 32:
        whole = mm_tn(x, d).astype(BF).reshape(n, 2 if split else 1, -1, out)
        halves = (place[1], 1 - place[1]) if split else (0,)
        return [lax.dynamic_index_in_dim(whole, h, 1, keepdims=False) for h in halves]
    size = group // 2 if split else group
    count = 2 if split else 1
    return pl.pallas_call(
        lambda *refs: grad_kernel(group, split, *refs),
        grid=(cols // block,),
        out_shape=(sized((n, size, out), BF),) * count,
        in_specs=[SCALARS, pl.BlockSpec((rows, block), lambda i: (0, i)), VMEM],
        out_specs=(pl.BlockSpec((block // group, size, out), lambda i: (i, 0, 0)),) * count,
        scratch_shapes=[pltpu.VMEM((block, out), F32)],
        compiler_params=params(),
        cost_estimate=cost(2 * rows * cols * out, 2 * (rows * (cols + out) + cols * out)),
    )(place, x, d)


def finish_kernel(blocks, sizes, place, *refs):
    pieces, out_refs = refs[:4], refs[4:]
    half = pieces[0].shape[0]
    row = [pl.multiple_of(part * half, 8) for part in (place[1], 1 - place[1])]
    for c in range(2):
        core = place[0] if c == 0 else 1 - place[0]
        for r in range(2):
            start = 0
            for out_ref, count, block in zip(out_refs, blocks, sizes):
                for b in range(count):
                    at = pl.multiple_of((2 * b + core) * block, 128)
                    got = pieces[2 * c + r][:, start : start + block].astype(F32)
                    out_ref[pl.ds(row[r], half), pl.ds(at, block)] = got
                    start += block


def finish(pieces, blocks, place):
    half, cols = pieces[0].shape
    sizes = [cols // sum(blocks)] * len(blocks)
    if half % 16 or sizes[0] % 128:
        def order(mine, there):
            return jnp.where(place[1] == 0, jnp.concatenate([mine, there]), jnp.concatenate([there, mine]))

        here, there = (order(*p).reshape(2 * half, sum(blocks), -1) for p in (pieces[:2], pieces[2:]))
        pair = [jnp.where(place[0] == 0, here, there), jnp.where(place[0] == 0, there, here)]
        whole = jnp.stack(pair, 2).astype(F32)
        got, start = [], 0
        for count in blocks:
            got.append(whole[:, start : start + count].reshape(2 * half, -1))
            start += count
        return got
    return pl.pallas_call(
        lambda *refs: finish_kernel(blocks, sizes, *refs),
        out_shape=tuple(sized((2 * half, 2 * count * size), F32) for count, size in zip(blocks, sizes)),
        in_specs=[SCALARS] + [VMEM] * 4,
        out_specs=(VMEM,) * len(blocks),
        compiler_params=params(),
        cost_estimate=cost(0, 24 * half * cols),
    )(place, *pieces)


def embed_time(timestep, width):
    half = width // 2
    frequency = jnp.exp(-math.log(10000.0) * jnp.arange(half, dtype=F32) / half)
    angles = timestep.astype(F32)[:, None] * frequency[None, :]
    return jnp.concatenate([jnp.cos(angles), jnp.sin(angles)], axis=1)


def normalize(v):
    centered = v - jnp.mean(v, axis=-1, keepdims=True)
    inv_std = lax.rsqrt(jnp.mean(centered * centered, axis=-1, keepdims=True) + EPS)
    return centered * inv_std, inv_std


def normalize_back(u, normed, inv_std):
    return inv_std * (
        u
        - jnp.mean(u, axis=-1, keepdims=True)
        - normed * jnp.mean(u * normed, axis=-1, keepdims=True)
    )


ROOT = math.sqrt(2.0 / math.pi)


def gelu(v):
    return 0.5 * v * (1.0 + jnp.tanh(ROOT * (v + 0.044715 * (v * v * v))))


def gelu_slope(v):
    t = jnp.tanh(ROOT * (v + 0.044715 * (v * v * v)))
    inner = ROOT * (1.0 + 3.0 * 0.044715 * (v * v))
    return 0.5 * (1.0 + t) + 0.5 * v * (1.0 - t * t) * inner


def lanes_of(shape, which):
    lane = lax.broadcasted_iota(jnp.int32, shape, 1)
    return (lane < HD) if which == 0 else (lane >= HD)


def softmax_rows(s):
    e = jnp.exp(s - jnp.max(s, axis=-1, keepdims=True))
    return e / jnp.sum(e, axis=-1, keepdims=True)


def keep_head(pair, which):
    return jnp.where(lanes_of(pair.shape, which), pair, jnp.zeros_like(pair))


def attend_kernel(h_ref, mod_ref, w_ref, qkv_ref, att_ref, in_ref=None):
    h = h_ref[0].astype(F32)
    normed, _ = normalize(h)
    x = (normed * (1.0 + mod_ref[0, 1:2, :]) + mod_ref[0, 0:1, :]).astype(BF)
    if in_ref is not None:
        in_ref[0] = x
    cols = qkv_ref.shape[2] // 3
    for part in range(3):
        qkv_ref[0, :, part * cols : (part + 1) * cols] = mm(
            x, w_ref[:, part * cols : (part + 1) * cols]
        ).astype(BF)
    for pair in range(cols // (2 * HD)):
        at = pair * 2 * HD
        q = qkv_ref[0, :, at : at + 2 * HD]
        k = qkv_ref[0, :, cols + at : cols + at + 2 * HD]
        v = qkv_ref[0, :, 2 * cols + at : 2 * cols + at + 2 * HD]
        total = None
        for which in range(2):
            s = mm_nt(keep_head(q, which), k) * (1.0 / math.sqrt(HD))
            o = mm(softmax_rows(s).astype(BF), keep_head(v, which))
            total = o if total is None else total + o
        att_ref[0, :, at : at + 2 * HD] = total.astype(BF)


def row_spec(tokens, width):
    return pl.BlockSpec((1, tokens, width), lambda i: (i, 0, 0))


def mod_spec(parts, width):
    return pl.BlockSpec((1, parts, width), lambda i: (i, 0, 0))


def attend(h, mods, wqkv, keep):
    latents, tokens, width = h.shape
    cols = 3 * width // 2
    outs = [(cols, BF), (cols // 3, BF)] + ([(width, BF)] if keep else [])
    return pl.pallas_call(
        attend_kernel,
        grid=(latents,),
        out_shape=tuple(sized((latents, tokens, c), t) for c, t in outs),
        in_specs=[row_spec(tokens, width), mod_spec(6, width), VMEM],
        out_specs=tuple(row_spec(tokens, c) for c, _ in outs),
        compiler_params=params(),
        cost_estimate=cost(latents * tokens * (2 * width * cols + 8 * tokens * cols), 8 << 20),
    )(h, mods, wqkv)


CHUNK = 512


def mlp_kernel(place, h_ref, mod_ref, own_ref, other_ref, wout_ref, wup_ref, wdown_ref,
               part_ref, midway_ref, proj_ref=None, in_ref=None, pre_ref=None, hidden_ref=None):
    half = own_ref.shape[2]
    low = place[0]
    projected = mm(own_ref[0], wout_ref[pl.ds(pl.multiple_of(low * half, 128), half), :])
    projected += mm(other_ref[0], wout_ref[pl.ds(pl.multiple_of((1 - low) * half, 128), half), :])
    midway = h_ref[0].astype(F32) + mod_ref[0, 2:3, :] * projected
    midway_ref[0] = midway
    normed, _ = normalize(midway)
    x = (normed * (1.0 + mod_ref[0, 4:5, :]) + mod_ref[0, 3:4, :]).astype(BF)
    if proj_ref is not None:
        proj_ref[0] = projected.astype(BF)
        in_ref[0] = x
    total = None
    for at in range(0, wup_ref.shape[1], CHUNK):
        pre = mm(x, wup_ref[:, at : at + CHUNK])
        hidden = gelu(pre).astype(BF)
        if pre_ref is not None:
            pre_ref[0, :, at : at + CHUNK] = pre
            hidden_ref[0, :, at : at + CHUNK] = hidden
        part = mm(hidden, wdown_ref[at : at + CHUNK, :])
        total = part if total is None else total + part
    part_ref[0] = total.astype(BF)


def mlp(place, h, mods, own, other, wout, wup, wdown, keep):
    latents, tokens, width = h.shape
    units = wup.shape[1]
    half = own.shape[2]
    outs = [(width, BF), (width, F32)]
    if keep:
        outs += [(width, BF), (width, BF), (units, F32), (units, BF)]
    return pl.pallas_call(
        mlp_kernel,
        grid=(latents,),
        out_shape=tuple(sized((latents, tokens, c), t) for c, t in outs),
        in_specs=[SCALARS, row_spec(tokens, width), mod_spec(6, width), row_spec(tokens, half),
                  row_spec(tokens, half), VMEM, VMEM, VMEM],
        out_specs=tuple(row_spec(tokens, c) for c, _ in outs),
        compiler_params=params(),
        cost_estimate=cost(latents * tokens * 2 * width * (2 * units + width), 16 << 20),
    )(place, h, mods, own, other, wout, wup, wdown)


def mlp_back_kernel(g_ref, mod_ref, pre_ref, wdown_ref, wup_ref, part_ref, d_pre_ref):
    d_mlp = (mod_ref[0, 5:6, :] * g_ref[0].astype(F32)).astype(BF)
    total = None
    for at in range(0, wup_ref.shape[1], CHUNK):
        d_hidden = mm_nt(d_mlp, wdown_ref[at : at + CHUNK, :])
        d_pre = (d_hidden * gelu_slope(pre_ref[0, :, at : at + CHUNK])).astype(BF)
        d_pre_ref[0, :, at : at + CHUNK] = d_pre
        part = mm_nt(d_pre, wup_ref[:, at : at + CHUNK])
        total = part if total is None else total + part
    part_ref[0] = total.astype(BF)


def mlp_back(g, mods, pre, wdown, wup):
    latents, tokens, width = g.shape
    units = wup.shape[1]
    return pl.pallas_call(
        mlp_back_kernel,
        grid=(latents,),
        out_shape=(sized((latents, tokens, width), BF), sized((latents, tokens, units), BF)),
        in_specs=[row_spec(tokens, width), mod_spec(6, width), row_spec(tokens, units), VMEM, VMEM],
        out_specs=(row_spec(tokens, width), row_spec(tokens, units)),
        compiler_params=params(),
        cost_estimate=cost(latents * tokens * 4 * width * units, 14 << 20),
    )(g, mods, pre, wdown, wup)


def attend_back_kernel(place, own_ref, other_ref, g_ref, midway_ref, proj_ref, mod_ref, qkv_ref,
                       wout_ref, wqkv_ref, part_ref, d_mid_ref, d_proj_ref, d_qkv_ref, sums_ref):
    d_in = own_ref[0].astype(F32) + other_ref[0].astype(F32)
    normed, inv_std = normalize(midway_ref[0])
    sums_ref[0, 1:2, :] = jnp.sum(d_in, axis=0, keepdims=True)
    sums_ref[0, 2:3, :] = jnp.sum(d_in * normed, axis=0, keepdims=True)
    d_mid = g_ref[0].astype(F32) + normalize_back(d_in * (1.0 + mod_ref[0, 4:5, :]), normed, inv_std)
    d_mid_ref[0] = d_mid
    d_proj = (mod_ref[0, 2:3, :] * d_mid).astype(BF)
    d_proj_ref[0] = d_proj
    sums_ref[0, 0:1, :] = jnp.sum(d_mid * proj_ref[0].astype(F32), axis=0, keepdims=True)
    cols = d_qkv_ref.shape[2] // 3
    low = place[0]
    d_att = mm_nt(d_proj, wout_ref[pl.ds(pl.multiple_of(low * cols, 128), cols), :]).astype(BF)
    scale = 1.0 / math.sqrt(HD)
    for pair in range(cols // (2 * HD)):
        at = pair * 2 * HD
        q = qkv_ref[0, :, at : at + 2 * HD]
        k = qkv_ref[0, :, cols + at : cols + at + 2 * HD]
        v = qkv_ref[0, :, 2 * cols + at : 2 * cols + at + 2 * HD]
        d_o = d_att[:, at : at + 2 * HD]
        dq = dk = dv = 0.0
        for which in range(2):
            q_one, d_one = keep_head(q, which), keep_head(d_o, which)
            probs = softmax_rows(mm_nt(q_one, k) * scale)
            d_probs = mm_nt(d_one, v)
            delta = jnp.sum(probs * d_probs, axis=-1, keepdims=True)
            d_s = (probs * (d_probs - delta)).astype(BF)
            dq += mm(d_s, keep_head(k, which))
            dk += mm_tn(d_s, q_one)
            dv += mm_tn(probs.astype(BF), d_one)
        d_qkv_ref[0, :, at : at + 2 * HD] = (dq * scale).astype(BF)
        d_qkv_ref[0, :, cols + at : cols + at + 2 * HD] = (dk * scale).astype(BF)
        d_qkv_ref[0, :, 2 * cols + at : 2 * cols + at + 2 * HD] = dv.astype(BF)
    part_ref[0] = mm_nt(d_qkv_ref[0], wqkv_ref[:, : 3 * cols]).astype(BF)


def attend_back(place, own, other, g, midway, projected, mods, qkv, wout, wqkv):
    latents, tokens, width = g.shape
    cols = qkv.shape[2]
    rows = row_spec(tokens, width)
    return pl.pallas_call(
        attend_back_kernel,
        grid=(latents,),
        out_shape=(
            sized(g.shape, BF),
            sized(g.shape, F32),
            sized(g.shape, BF),
            sized((latents, tokens, cols), BF),
            sized((latents, 3, width), F32),
        ),
        in_specs=[SCALARS, rows, rows, rows, rows, rows, mod_spec(6, width), row_spec(tokens, cols), VMEM, VMEM],
        out_specs=(rows, rows, rows, row_spec(tokens, cols), mod_spec(3, width)),
        compiler_params=params(),
        cost_estimate=cost(latents * tokens * (2 * width * cols + 20 * tokens * cols), 14 << 20),
    )(place, own, other, g, midway, projected, mods, qkv, wout, wqkv)


def inputs_back_kernel(own_ref, other_ref, h_ref, d_mid_ref, mod_ref, d_h_ref, sums_ref):
    d_in = own_ref[0].astype(F32) + other_ref[0].astype(F32)
    normed, inv_std = normalize(h_ref[0].astype(F32))
    sums_ref[0, 0:1, :] = jnp.sum(d_in, axis=0, keepdims=True)
    sums_ref[0, 1:2, :] = jnp.sum(d_in * normed, axis=0, keepdims=True)
    d_h = d_mid_ref[0] + normalize_back(d_in * (1.0 + mod_ref[0, 1:2, :]), normed, inv_std)
    d_h_ref[0] = d_h.astype(d_h_ref.dtype)


def inputs_back(own, other, h, d_mid, mods, dtype):
    latents, tokens, width = h.shape
    rows = row_spec(tokens, width)
    return pl.pallas_call(
        inputs_back_kernel,
        grid=(latents,),
        out_shape=(sized(h.shape, dtype), sized((latents, 2, width), F32)),
        in_specs=[rows, rows, rows, rows, mod_spec(6, width)],
        out_specs=(rows, mod_spec(2, width)),
        compiler_params=params(),
        cost_estimate=cost(0, 10 << 20),
    )(own, other, h, d_mid, mods)


def body(boundary, timestep, label, label_table, ada_weight, qkv_weight, out_weight, up_weight, down_weight):
    on_first = lax.axis_index("section") == 0
    seq = lax.axis_index("seq")
    low, high = seq % 2, seq // 2
    fsdp = lax.axis_index("fsdp")
    n_seq, n_fsdp, n_sec = lax.axis_size("seq"), lax.axis_size("fsdp"), lax.axis_size("section")
    assert n_seq == 4
    place = jnp.stack([low, high, fsdp]).astype(jnp.int32)
    width = boundary.shape[-1]
    tokens_here = boundary.shape[2]
    latents = boundary.shape[1] // 2
    ada, wqkv, wout, wup, wdown = (a[0] for a in (ada_weight, qkv_weight, out_weight, up_weight, down_weight))
    share = wqkv.shape[0]

    def by_core(here, there):
        return jnp.where(low == 0, here, there), jnp.where(low == 0, there, here)

    attn_own, attn_mine = pick_columns((wqkv, wout), (3, 1), place)
    up_own, up_mine = pick_columns((wup,), (n_fsdp,), place)
    sub = wdown.shape[0] // 2
    down_own = lax.dynamic_slice_in_dim(wdown, low * sub, sub, 0)
    down_mine = lax.dynamic_slice_in_dim(wdown, low * sub + high * (sub // 2), sub // 2, 0)

    own = boundary[0]
    stay = lax.dynamic_slice_in_dim(own, high * latents, latents, 0)
    leave = lax.dynamic_slice_in_dim(own, (1 - high) * latents, latents, 0)
    leave = y_swap(after(leave, attn_mine))

    cond = embed_time(timestep, width) + jnp.take(label_table, label, axis=0).astype(F32)
    silu_cond = jax.nn.silu(cond).astype(BF)
    silu_all = gather_back(after(silu_cond, attn_mine, up_mine), "fsdp")
    rest = {}

    def between(k, i, token):
        if (k, i) == (1, 0):
            cols = lax.dynamic_slice_in_dim(together(silu_all, token), fsdp * share, share, 2)
            mine = lax.dynamic_slice_in_dim(cols, high * latents, latents, 1)
            parts = mm(mine.reshape(-1, share), ada).reshape(n_fsdp, latents, -1)
            rest["silu_cols"] = cols.reshape(-1, share)
            rest["mods"] = send_back(parts, "fsdp")
            half = jnp.concatenate([stay, after(leave, parts)], axis=1)
            rest["rows"] = jnp.concatenate(by_core(half, core_swap(half)), axis=1)
            return parts
        if (k, i) == (2, 2):
            mods = jnp.sum(together(rest["mods"], token), axis=0)
            rest["mods"] = mods.reshape(latents, 6, width)
            return mods
        return token

    full_attn, full_up, full_down = whole_weights(
        (attn_own, up_own, down_own), (attn_mine, up_mine, down_mine), place, between
    )
    full_qkv = full_attn
    full_out = join_cores(full_attn, width // 2, place)
    silu_cols, mods, own_rows = rest["silu_cols"], rest["mods"], rest["rows"]

    def cross(rows, step):
        half_tokens = rows.shape[1] // 2
        mine = lax.dynamic_slice_in_dim(rows, low * half_tokens, half_tokens, 1)
        route = [(i, i + step) for i in range(n_sec) if 0 <= i + step < n_sec]
        here = lax.ppermute(mine, "section", route)
        return jnp.concatenate(by_core(here, core_swap(here)), axis=1)

    gate_two = mods[:, 5:6]

    _, att = attend(own_rows, mods, full_qkv, False)
    part, midway = mlp(place, own_rows, mods, att, core_swap(att), full_out, full_up, full_down, False)
    mlp_out = part.astype(F32) + core_swap(part).astype(F32)
    passed = cross((midway + gate_two * mlp_out).astype(BF), 1)

    h = jnp.where(on_first, own_rows, passed)
    qkv, att, attn_in = attend(h, mods, full_qkv, True)
    att_other = core_swap(att)
    part, midway, projected, mlp_in, pre, hidden = mlp(
        place, h, mods, att, att_other, full_out, full_up, full_down, True
    )
    mlp_out = part.astype(F32) + core_swap(part).astype(F32)
    layer_out = midway + gate_two * mlp_out

    back_part, _ = mlp_back(own_rows, mods, pre, full_down, full_up)
    part_two, d_mid, _, _, _ = attend_back(
        place, back_part, core_swap(back_part), own_rows, midway, projected, mods, qkv, full_out, full_qkv
    )
    first_d_h, _ = inputs_back(part_two, core_swap(part_two), h, d_mid, mods, BF)
    incoming = cross(first_d_h, -1)

    def flat(a):
        return a.reshape(-1, a.shape[-1])

    ring = small(n_fsdp)

    def ring_start(blocks):
        return shift(ring_block(blocks, 1), "fsdp", 1)

    def scatter(blocks):
        return lax.psum_scatter(blocks, "fsdp", scatter_dimension=0, tiled=False)

    def y_add(mine, there):
        return (mine.astype(F32) + there.astype(F32)).astype(BF)

    g = jnp.where(on_first, incoming, own_rows)
    d_mlp = (gate_two * g.astype(F32)).astype(BF)
    back_part, d_pre = mlp_back(g, mods, pre, full_down, full_up)
    back_there = core_swap(back_part)
    up_mine, up_other = weight_grad(flat(mlp_in), flat(d_pre), place, True)
    up_there = y_swap(up_other)
    (down,) = weight_grad(flat(hidden), after(flat(d_mlp), up_mine), place, False)
    runs = {}

    def begin(name, blocks):
        runs[name] = (blocks, ring_start(blocks) if ring else None)
        return blocks

    def step(name, back, token):
        blocks, run = runs[name]
        if not ring:
            return scatter(blocks) if back == n_fsdp else blocks
        part = ring_add(blocks, back, after(run, token))
        if back < n_fsdp:
            runs[name] = (blocks, shift(part, "fsdp", 1))
        return part

    begin("down", down)
    part_two, d_mid, d_proj, d_qkv, sums_mid = attend_back(
        place, after(back_part, down), back_there, g, midway, projected, mods, qkv, full_out, full_qkv
    )
    two_there = core_swap(part_two)
    last = step("down", 2, part_two)
    qkv_mine, qkv_other = weight_grad(flat(attn_in), after(flat(d_qkv), last), place, True)
    cols = width // 2
    own_cols = lax.dynamic_slice_in_dim(flat(d_proj), low * cols, cols, 1)
    attended = jnp.concatenate(by_core(flat(att), flat(att_other)), axis=1)
    out_mine, out_other = weight_grad(after(attended, qkv_mine), own_cols, place, True)
    attn_mine = jnp.concatenate([qkv_mine, out_mine], axis=2)
    attn_there = y_swap(jnp.concatenate([qkv_other, out_other], axis=2))
    d_h, sums_in = inputs_back(after(part_two, attn_mine), two_there, h, d_mid, mods, F32)
    last = begin("up", y_add(up_mine, after(up_there, d_h)))
    last = step("down", 3, last)
    last = step("up", 2, last)

    d_gate_two = jnp.sum(g.astype(F32) * mlp_out, axis=1)
    d_mod = jnp.concatenate([part.reshape(latents, -1) for part in (sums_in, sums_mid, d_gate_two)], axis=1)
    d_mine = after(d_mod.astype(BF), last)
    d_there = y_swap(d_mine)
    last = begin("attn", y_add(attn_mine, after(attn_there, d_mine)))
    last = down_part = step("down", 4 if ring else n_fsdp, last)
    down_there = y_swap(down_part)
    last = step("up", 3, last)
    d_there = after(d_there, last)
    d_six = jnp.where(
        high == 0, jnp.concatenate([d_mine, d_there]), jnp.concatenate([d_there, d_mine])
    )
    d_all = gather_back(after(d_six, last), "fsdp")
    last = step("attn", 2, last)
    last = up_part = step("up", 4 if ring else n_fsdp, last)
    up_last, up_core = y_swap(up_part), core_swap(up_part)
    d_all = together(d_all, last).reshape(-1, d_six.shape[1])
    d_silu = mm_nt(d_all, ada).reshape(n_fsdp, 2 * latents, share)
    d_silu = send_back(d_silu, "fsdp")
    last = step("attn", 3, last)
    ada_cols = ada.shape[1] // n_seq
    g_ada = mm_tn(silu_cols, lax.dynamic_slice_in_dim(after(d_all, last), seq * ada_cols, ada_cols, 1))
    last = attn_part = step("attn", 4 if ring else n_fsdp, last)
    attn_last, attn_core = y_swap(attn_part), core_swap(attn_part)

    d_silu = together(d_silu, last)
    ordered = jnp.concatenate([d_silu, d_silu[:-1]])
    d_silu = lax.dynamic_slice_in_dim(ordered, (n_fsdp - fsdp) % n_fsdp, n_fsdp, 0)
    d_silu = d_silu.transpose(1, 0, 2).reshape(2 * latents, width)
    cond_grad = jax.vjp(jax.nn.silu, cond)[1](d_silu)[0]

    down_sum = y_add(down_part, down_there)
    g_down = jnp.concatenate(by_core(down_sum, core_swap(down_sum))).astype(F32)
    g_up = finish((up_part, up_last, up_core, core_swap(up_last)), (n_fsdp,), place)[0]
    g_qkv, g_out = finish((attn_part, attn_last, attn_core, core_swap(attn_last)), (3, 1), place)

    result = jnp.where(on_first, d_h, layer_out)
    blocks = result.reshape(latents, 2, 2, tokens_here, width)
    blocks = lax.dynamic_index_in_dim(blocks, low, 1, keepdims=False)
    keep = blocks[:, 0]
    arrive = after(y_swap(blocks[:, 1].astype(BF)), attn_part).astype(F32)
    end_rows = jnp.where(
        high == 0, jnp.concatenate([keep, arrive], axis=0), jnp.concatenate([arrive, keep], axis=0)
    )
    return (
        end_rows[None],
        cond_grad[None],
        g_ada[None],
        g_qkv[None],
        g_out[None],
        g_up[None],
        g_down[None],
    )


def solution(mesh):
    rows = P("section", "fsdp", "seq", None)
    weight = P("section", "fsdp", None)
    return jax.shard_map(
        body,
        mesh=mesh,
        in_specs=(rows, P("fsdp"), P("fsdp"), P(), weight, weight, weight, weight, weight),
        out_specs=(rows, weight, P("section", "fsdp", "seq"), weight, weight, weight, weight),
        check_vma=False,
    )
```

```python
import math

import jax
import jax.numpy as jnp
from jax import lax
from jax.experimental import pallas as pl
from jax.experimental.pallas import tpu as pltpu
from jax.sharding import PartitionSpec as P

HD = 64
EPS = 1e-06
BF = jnp.bfloat16
F32 = jnp.float32


def dot(a, b, dims):
    return lax.dot_general(a, b, (dims, ((), ())), preferred_element_type=F32)


def mm(a, b):
    return dot(a, b, ((1,), (0,)))


def mm_nt(a, b):
    return dot(a, b, ((1,), (1,)))


def mm_tn(a, b):
    return dot(a, b, ((0,), (0,)))


def after(x, *tokens):
    return lax.optimization_barrier((x,) + tokens)[0]


def core_swap(x):
    return lax.ppermute(x, "seq", [(i, i ^ 1) for i in range(lax.axis_size("seq"))])


def y_swap(x):
    return lax.ppermute(x, "seq", [(i, i ^ 2) for i in range(lax.axis_size("seq"))])


def shift(x, axis, distance):
    n = lax.axis_size(axis)
    return lax.ppermute(x, axis, [(i, (i + distance) % n) for i in range(n)])


def small(n):
    return n == 4


def gather_back(x, axis):
    n = lax.axis_size(axis)
    if not small(n):
        whole = jnp.flip(lax.all_gather(x, axis), 0)
        doubled = jnp.concatenate([whole, whole])
        whole = lax.dynamic_slice_in_dim(doubled, n - 1 - lax.axis_index(axis), n, 0)
        return [whole[k] for k in range(n)]
    return [x] + [shift(x, axis, k) for k in range(1, n)]


def send_back(x, axis):
    n = lax.axis_size(axis)
    if not small(n):
        me = lax.axis_index(axis)
        doubled = jnp.concatenate([x, x])
        whole = jnp.flip(lax.dynamic_slice_in_dim(doubled, (me + 1) % n, n, 0), 0)
        got = lax.all_to_all(whole, axis, split_axis=0, concat_axis=0, tiled=True)
        got = lax.dynamic_slice_in_dim(jnp.concatenate([got, got]), me, n, 0)
        return [got[k] for k in range(n)]
    return [x[0]] + [shift(x[k], axis, n - k) for k in range(1, n)]


def together(pieces, token):
    return jnp.stack(lax.optimization_barrier(tuple(pieces) + (token,))[:-1])


ANY = pl.BlockSpec(memory_space=pl.ANY)
SCALARS = pl.BlockSpec(memory_space=pltpu.SMEM)
VMEM = pl.BlockSpec(memory_space=pltpu.VMEM)


def params(mib=26):
    return pltpu.CompilerParams(vmem_limit_bytes=mib << 20)


def cost(flops, moved):
    return pl.CostEstimate(flops=int(flops), bytes_accessed=int(moved), transcendentals=0)


def sized(shape, dtype):
    return jax.ShapeDtypeStruct(shape, dtype)


def pick_kernel(blocks, place, *refs):
    w_refs, (own_ref, mine_ref) = refs[:-2], refs[-2:]
    at = 0
    for w_ref, count in zip(w_refs, blocks):
        block = w_ref.shape[1] // count // 2
        for b in range(count):
            start = pl.multiple_of((2 * b + place[0]) * block, 128)
            own_ref[:, at : at + block] = w_ref[:, pl.ds(start, block)]
            at += block
    half = mine_ref.shape[0]
    mine_ref[...] = own_ref[pl.ds(pl.multiple_of(place[1] * half, 16), half), :]


def pick_columns(ws, blocks, place):
    rows = ws[0].shape[0]
    half = rows // 2
    sizes = [w.shape[1] // count // 2 for w, count in zip(ws, blocks)]
    if half % 16 or any(size % 128 for size in sizes):
        own = jnp.concatenate(
            [
                lax.dynamic_index_in_dim(w.reshape(rows, count, 2, -1), place[0], 2, keepdims=False).reshape(rows, -1)
                for w, count in zip(ws, blocks)
            ],
            axis=1,
        )
        return own, lax.dynamic_slice_in_dim(own, place[1] * half, half, 0)
    cols = sum(w.shape[1] for w in ws) // 2
    return pl.pallas_call(
        lambda *refs: pick_kernel(blocks, *refs),
        out_shape=(sized((rows, cols), BF), sized((half, cols), BF)),
        in_specs=[SCALARS] + [VMEM] * len(ws),
        out_specs=(VMEM, VMEM),
        compiler_params=params(),
        cost_estimate=cost(0, 8 * rows * cols),
    )(place, *ws)


def assemble_kernel(n, share, place, own_ref, *refs):
    mine_refs, other_refs, out_ref, sems = refs[: n - 1], refs[n - 1 : 2 * n - 2], refs[-2], refs[-1]
    half = share // 2
    me = place[2]

    def rows(start, size):
        return out_ref.at[pl.ds(pl.multiple_of(start, 16), size)]

    copies = [pltpu.make_async_copy(own_ref, rows(me * share, share), sems.at[0])]
    for k in range(1, n):
        base = lax.rem(me - k + n, n) * share
        for j, (ref, part) in enumerate(((mine_refs[k - 1], place[1]), (other_refs[k - 1], 1 - place[1]))):
            copies.append(
                pltpu.make_async_copy(ref, rows(base + part * half, half), sems.at[2 * k - 1 + j])
            )
    for copy in copies:
        copy.start()
    for copy in copies:
        copy.wait()


def assemble(own, mine, other, place):
    n = len(mine) + 1
    share = own.shape[0]
    return pl.pallas_call(
        lambda *refs: assemble_kernel(n, share, *refs),
        out_shape=sized((n * share, own.shape[1]), own.dtype),
        in_specs=[SCALARS] + [ANY] * (2 * n - 1),
        out_specs=ANY,
        scratch_shapes=[pltpu.SemaphoreType.DMA((2 * n - 1,))],
        compiler_params=params(),
        cost_estimate=cost(0, 2 * n * share * own.shape[1] * 2),
    )(place, own, *mine, *other)


def whole_weights(owns, mines, place, between):
    n = lax.axis_size("fsdp")
    if not small(n):
        between(1, 0, mines[0])
        between(2, 2, mines[0])
        whole = []
        for own, mine in zip(owns, mines):
            here = lax.all_gather(mine, "fsdp")
            there = y_swap(here)
            pair = jnp.where(place[1] == 0, jnp.stack([here, there], 1), jnp.stack([there, here], 1))
            whole.append(pair.reshape(n * own.shape[0], own.shape[1]))
        return whole
    runs = [shift(mine, "fsdp", 1) for mine in mines]
    arrived, there = [[] for _ in mines], [[] for _ in mines]
    last, swaps = mines[0], []
    for k in range(1, n):
        for i in range(len(runs)):
            block = after(runs[i], last, *swaps[-2:-1])
            arrived[i].append(block)
            if k < n - 1:
                runs[i] = shift(block, "fsdp", 1)
            swaps.append(y_swap(block))
            there[i].append(swaps[-1])
            last = between(k, i, block)
    return [assemble(*four, place) for four in zip(owns, arrived, there)]


def join_kernel(place, here_ref, there_ref, out_ref):
    cols = there_ref.shape[1]
    here = here_ref[:, here_ref.shape[1] - cols :]
    out_ref[:, pl.ds(pl.multiple_of(place[0] * cols, 128), cols)] = here
    out_ref[:, pl.ds(pl.multiple_of((1 - place[0]) * cols, 128), cols)] = there_ref[...]


def join_cores(here, cols, place):
    rows = here.shape[0]
    there = core_swap(here[:, here.shape[1] - cols :])
    return pl.pallas_call(
        join_kernel,
        out_shape=sized((rows, 2 * cols), here.dtype),
        in_specs=[SCALARS, VMEM, VMEM],
        out_specs=VMEM,
        compiler_params=params(),
        cost_estimate=cost(0, 8 * rows * cols),
    )(place, here, there)


def ring_block(blocks, back):
    n = lax.axis_size("fsdp")
    return lax.dynamic_index_in_dim(blocks, (lax.axis_index("fsdp") + n - back) % n, 0, keepdims=False)


def ring_add(blocks, back, arrived):
    return (ring_block(blocks, back).astype(F32) + arrived.astype(F32)).astype(BF)


def grad_kernel(group, split, place, x_ref, d_ref, *refs):
    out_refs, whole_ref = refs[:-1], refs[-1]
    whole_ref[...] = mm_tn(x_ref[...], d_ref[...])
    size = out_refs[0].shape[1]
    for z in range(out_refs[0].shape[0]):
        for ref, part in zip(out_refs, (place[1], 1 - place[1]) if split else (0,)):
            start = pl.multiple_of(z * group + part * size, 8)
            ref[z] = whole_ref[pl.ds(start, size), :].astype(BF)


def weight_grad(x, d, place, split):
    n = lax.axis_size("fsdp")
    rows, cols = x.shape
    out = d.shape[1]
    group = cols // n
    block = min(cols, 384)
    if group > block or block % group or cols % block or group % 32:
        whole = mm_tn(x, d).astype(BF).reshape(n, 2 if split else 1, -1, out)
        halves = (place[1], 1 - place[1]) if split else (0,)
        return [lax.dynamic_index_in_dim(whole, h, 1, keepdims=False) for h in halves]
    size = group // 2 if split else group
    count = 2 if split else 1
    return pl.pallas_call(
        lambda *refs: grad_kernel(group, split, *refs),
        grid=(cols // block,),
        out_shape=(sized((n, size, out), BF),) * count,
        in_specs=[SCALARS, pl.BlockSpec((rows, block), lambda i: (0, i)), VMEM],
        out_specs=(pl.BlockSpec((block // group, size, out), lambda i: (i, 0, 0)),) * count,
        scratch_shapes=[pltpu.VMEM((block, out), F32)],
        compiler_params=params(),
        cost_estimate=cost(2 * rows * cols * out, 2 * (rows * (cols + out) + cols * out)),
    )(place, x, d)


def finish_kernel(blocks, sizes, place, *refs):
    pieces, out_refs = refs[:4], refs[4:]
    half = pieces[0].shape[0]
    row = [pl.multiple_of(part * half, 8) for part in (place[1], 1 - place[1])]
    for c in range(2):
        core = place[0] if c == 0 else 1 - place[0]
        for r in range(2):
            start = 0
            for out_ref, count, block in zip(out_refs, blocks, sizes):
                for b in range(count):
                    at = pl.multiple_of((2 * b + core) * block, 128)
                    got = pieces[2 * c + r][:, start : start + block].astype(F32)
                    out_ref[pl.ds(row[r], half), pl.ds(at, block)] = got
                    start += block


def finish(pieces, blocks, place):
    half, cols = pieces[0].shape
    sizes = [cols // sum(blocks)] * len(blocks)
    if half % 16 or sizes[0] % 128:
        def order(mine, there):
            return jnp.where(place[1] == 0, jnp.concatenate([mine, there]), jnp.concatenate([there, mine]))

        here, there = (order(*p).reshape(2 * half, sum(blocks), -1) for p in (pieces[:2], pieces[2:]))
        pair = [jnp.where(place[0] == 0, here, there), jnp.where(place[0] == 0, there, here)]
        whole = jnp.stack(pair, 2).astype(F32)
        got, start = [], 0
        for count in blocks:
            got.append(whole[:, start : start + count].reshape(2 * half, -1))
            start += count
        return got
    return pl.pallas_call(
        lambda *refs: finish_kernel(blocks, sizes, *refs),
        out_shape=tuple(sized((2 * half, 2 * count * size), F32) for count, size in zip(blocks, sizes)),
        in_specs=[SCALARS] + [VMEM] * 4,
        out_specs=(VMEM,) * len(blocks),
        compiler_params=params(),
        cost_estimate=cost(0, 24 * half * cols),
    )(place, *pieces)


def embed_time(timestep, width):
    half = width // 2
    frequency = jnp.exp(-math.log(10000.0) * jnp.arange(half, dtype=F32) / half)
    angles = timestep.astype(F32)[:, None] * frequency[None, :]
    return jnp.concatenate([jnp.cos(angles), jnp.sin(angles)], axis=1)


def normalize(v):
    centered = v - jnp.mean(v, axis=-1, keepdims=True)
    inv_std = lax.rsqrt(jnp.mean(centered * centered, axis=-1, keepdims=True) + EPS)
    return centered * inv_std, inv_std


def normalize_back(u, normed, inv_std):
    return inv_std * (
        u
        - jnp.mean(u, axis=-1, keepdims=True)
        - normed * jnp.mean(u * normed, axis=-1, keepdims=True)
    )


ROOT = math.sqrt(2.0 / math.pi)


def gelu(v):
    square = v * v
    t = jnp.tanh(v * (ROOT + (ROOT * 0.044715) * square))
    half = 0.5 * v
    return half + half * t, t, half, square


def gelu_slope(t, half, square):
    inner = ROOT + (3.0 * 0.044715 * ROOT) * square
    return (0.5 + 0.5 * t) + (half * inner) * (1.0 - t * t)


def lanes_of(shape, which):
    lane = lax.broadcasted_iota(jnp.int32, shape, 1)
    return (lane < HD) if which == 0 else (lane >= HD)


def keep_head(pair, which):
    return jnp.where(lanes_of(pair.shape, which), pair, jnp.zeros_like(pair))


def keep_rows(pair, which):
    row = lax.broadcasted_iota(jnp.int32, pair.shape, 0)
    return jnp.where((row < HD) if which == 0 else (row >= HD), pair, jnp.zeros_like(pair))


def attend_kernel(h_ref, mod_ref, w_ref, qkv_ref, att_ref, in_ref=None, log_ref=None):
    h = h_ref[0].astype(F32)
    normed, _ = normalize(h)
    x = (normed * (1.0 + mod_ref[0, 1:2, :]) + mod_ref[0, 0:1, :]).astype(BF)
    if in_ref is not None:
        in_ref[0] = x
    cols = qkv_ref.shape[2] // 3
    for part in range(3):
        qkv_ref[0, :, part * cols : (part + 1) * cols] = mm(
            x, w_ref[:, part * cols : (part + 1) * cols]
        ).astype(BF)
    for pair in range(cols // (2 * HD)):
        at = pair * 2 * HD
        q = qkv_ref[0, :, at : at + 2 * HD] * (1.0 / math.sqrt(HD))
        k = qkv_ref[0, :, cols + at : cols + at + 2 * HD]
        v_t = qkv_ref[0, :, 2 * cols + at : 2 * cols + at + 2 * HD].T
        total = None
        for which in range(2):
            s_t = mm_nt(k, keep_head(q, which))
            top = jnp.max(s_t, axis=0, keepdims=True)
            e = jnp.exp(s_t - top)
            whole = jnp.sum(e, axis=0, keepdims=True)
            if log_ref is not None:
                log_ref[0, 2 * pair + which : 2 * pair + which + 1, :] = top + jnp.log(whole)
            o_t = mm(keep_rows(v_t, which), (e * (1.0 / whole)).astype(BF))
            total = o_t if total is None else total + o_t
        att_ref[0, :, at : at + 2 * HD] = total.astype(BF).T


def row_spec(tokens, width):
    return pl.BlockSpec((1, tokens, width), lambda i: (i, 0, 0))


def mod_spec(parts, width):
    return pl.BlockSpec((1, parts, width), lambda i: (i, 0, 0))


def attend(h, mods, wqkv, keep):
    latents, tokens, width = h.shape
    cols = 3 * width // 2
    outs = [(tokens, cols, BF), (tokens, cols // 3, BF)]
    if keep:
        outs += [(tokens, width, BF), (cols // 3 // HD, tokens, F32)]
    return pl.pallas_call(
        attend_kernel,
        grid=(latents,),
        out_shape=tuple(sized((latents, r, c), t) for r, c, t in outs),
        in_specs=[row_spec(tokens, width), mod_spec(6, width), VMEM],
        out_specs=tuple(row_spec(r, c) for r, c, _ in outs),
        compiler_params=params(),
        cost_estimate=cost(latents * tokens * (2 * width * cols + 8 * tokens * cols), 8 << 20),
    )(h, mods, wqkv)


CHUNK = 512


def mlp_kernel(place, h_ref, mod_ref, own_ref, other_ref, wout_ref, wup_ref, wdown_ref,
               part_ref, midway_ref, proj_ref=None, in_ref=None, slope_ref=None, hidden_ref=None):
    half = own_ref.shape[2]
    low = place[0]
    projected = mm(own_ref[0], wout_ref[pl.ds(pl.multiple_of(low * half, 128), half), :])
    projected += mm(other_ref[0], wout_ref[pl.ds(pl.multiple_of((1 - low) * half, 128), half), :])
    midway = h_ref[0].astype(F32) + mod_ref[0, 2:3, :] * projected
    midway_ref[0] = midway
    normed, _ = normalize(midway)
    x = (normed * (1.0 + mod_ref[0, 4:5, :]) + mod_ref[0, 3:4, :]).astype(BF)
    if proj_ref is not None:
        proj_ref[0] = projected.astype(BF)
        in_ref[0] = x
    total = None
    for at in range(0, wup_ref.shape[1], CHUNK):
        pre = mm(x, wup_ref[:, at : at + CHUNK])
        hidden, *rest = gelu(pre)
        hidden = hidden.astype(BF)
        if slope_ref is not None:
            slope_ref[0, :, at : at + CHUNK] = gelu_slope(*rest).astype(BF)
            hidden_ref[0, :, at : at + CHUNK] = hidden
        part = mm(hidden, wdown_ref[at : at + CHUNK, :])
        total = part if total is None else total + part
    part_ref[0] = total.astype(BF)


def mlp(place, h, mods, own, other, wout, wup, wdown, keep):
    latents, tokens, width = h.shape
    units = wup.shape[1]
    half = own.shape[2]
    outs = [(width, BF), (width, F32)]
    if keep:
        outs += [(width, BF), (width, BF), (units, BF), (units, BF)]
    return pl.pallas_call(
        mlp_kernel,
        grid=(latents,),
        out_shape=tuple(sized((latents, tokens, c), t) for c, t in outs),
        in_specs=[SCALARS, row_spec(tokens, width), mod_spec(6, width), row_spec(tokens, half),
                  row_spec(tokens, half), VMEM, VMEM, VMEM],
        out_specs=tuple(row_spec(tokens, c) for c, _ in outs),
        compiler_params=params(),
        cost_estimate=cost(latents * tokens * 2 * width * (2 * units + width), 16 << 20),
    )(place, h, mods, own, other, wout, wup, wdown)


def mlp_back_kernel(g_ref, mod_ref, slope_ref, wdown_ref, wup_ref, part_ref, d_pre_ref):
    d_mlp = (mod_ref[0, 5:6, :] * g_ref[0].astype(F32)).astype(BF)
    total = None
    for at in range(0, wup_ref.shape[1], CHUNK):
        d_hidden = mm_nt(d_mlp, wdown_ref[at : at + CHUNK, :])
        d_pre = (d_hidden * slope_ref[0, :, at : at + CHUNK].astype(F32)).astype(BF)
        d_pre_ref[0, :, at : at + CHUNK] = d_pre
        part = mm_nt(d_pre, wup_ref[:, at : at + CHUNK])
        total = part if total is None else total + part
    part_ref[0] = total.astype(BF)


def mlp_back(g, mods, slope, wdown, wup):
    latents, tokens, width = g.shape
    units = wup.shape[1]
    return pl.pallas_call(
        mlp_back_kernel,
        grid=(latents,),
        out_shape=(sized((latents, tokens, width), BF), sized((latents, tokens, units), BF)),
        in_specs=[row_spec(tokens, width), mod_spec(6, width), row_spec(tokens, units), VMEM, VMEM],
        out_specs=(row_spec(tokens, width), row_spec(tokens, units)),
        compiler_params=params(),
        cost_estimate=cost(latents * tokens * 4 * width * units, 14 << 20),
    )(g, mods, slope, wdown, wup)


def attend_back_kernel(place, own_ref, other_ref, g_ref, midway_ref, proj_ref, mod_ref, qkv_ref, log_ref,
                       wout_ref, wqkv_ref, part_ref, d_mid_ref, d_proj_ref, d_qkv_ref, sums_ref):
    d_in = own_ref[0].astype(F32) + other_ref[0].astype(F32)
    normed, inv_std = normalize(midway_ref[0])
    sums_ref[0, 1:2, :] = jnp.sum(d_in, axis=0, keepdims=True)
    sums_ref[0, 2:3, :] = jnp.sum(d_in * normed, axis=0, keepdims=True)
    d_mid = g_ref[0].astype(F32) + normalize_back(d_in * (1.0 + mod_ref[0, 4:5, :]), normed, inv_std)
    d_mid_ref[0] = d_mid
    d_proj = (mod_ref[0, 2:3, :] * d_mid).astype(BF)
    d_proj_ref[0] = d_proj
    sums_ref[0, 0:1, :] = jnp.sum(d_mid * proj_ref[0].astype(F32), axis=0, keepdims=True)
    cols = d_qkv_ref.shape[2] // 3
    low = place[0]
    d_att = mm_nt(d_proj, wout_ref[pl.ds(pl.multiple_of(low * cols, 128), cols), :]).astype(BF)
    scale = 1.0 / math.sqrt(HD)
    for pair in range(cols // (2 * HD)):
        at = pair * 2 * HD
        q = qkv_ref[0, :, at : at + 2 * HD] * scale
        k = qkv_ref[0, :, cols + at : cols + at + 2 * HD]
        v = qkv_ref[0, :, 2 * cols + at : 2 * cols + at + 2 * HD]
        k_t = k.T
        d_o = d_att[:, at : at + 2 * HD]
        dq_t = dk = dv = 0.0
        for which in range(2):
            q_one, d_one = keep_head(q, which), keep_head(d_o, which)
            log = log_ref[0, 2 * pair + which : 2 * pair + which + 1, :]
            probs_t = jnp.exp(mm_nt(k, q_one) - log)
            weighted = probs_t * mm_nt(v, d_one)
            delta = jnp.sum(weighted, axis=0, keepdims=True)
            d_s_t = (weighted - probs_t * delta).astype(BF)
            dq_t += mm(keep_rows(k_t, which), d_s_t)
            dk += mm(d_s_t, q_one)
            dv += mm(probs_t.astype(BF), d_one)
        d_qkv_ref[0, :, at : at + 2 * HD] = (dq_t * scale).astype(BF).T
        d_qkv_ref[0, :, cols + at : cols + at + 2 * HD] = dk.astype(BF)
        d_qkv_ref[0, :, 2 * cols + at : 2 * cols + at + 2 * HD] = dv.astype(BF)
    part_ref[0] = mm_nt(d_qkv_ref[0], wqkv_ref[:, : 3 * cols]).astype(BF)


def attend_back(place, own, other, g, midway, projected, mods, qkv, logs, wout, wqkv):
    latents, tokens, width = g.shape
    cols = qkv.shape[2]
    rows = row_spec(tokens, width)
    return pl.pallas_call(
        attend_back_kernel,
        grid=(latents,),
        out_shape=(
            sized(g.shape, BF),
            sized(g.shape, F32),
            sized(g.shape, BF),
            sized((latents, tokens, cols), BF),
            sized((latents, 3, width), F32),
        ),
        in_specs=[SCALARS, rows, rows, rows, rows, rows, mod_spec(6, width), row_spec(tokens, cols),
                  row_spec(logs.shape[1], tokens), VMEM, VMEM],
        out_specs=(rows, rows, rows, row_spec(tokens, cols), mod_spec(3, width)),
        compiler_params=params(),
        cost_estimate=cost(latents * tokens * (2 * width * cols + 20 * tokens * cols), 14 << 20),
    )(place, own, other, g, midway, projected, mods, qkv, logs, wout, wqkv)


def inputs_back_kernel(own_ref, other_ref, h_ref, d_mid_ref, mod_ref, d_h_ref, sums_ref):
    d_in = own_ref[0].astype(F32) + other_ref[0].astype(F32)
    normed, inv_std = normalize(h_ref[0].astype(F32))
    sums_ref[0, 0:1, :] = jnp.sum(d_in, axis=0, keepdims=True)
    sums_ref[0, 1:2, :] = jnp.sum(d_in * normed, axis=0, keepdims=True)
    d_h = d_mid_ref[0] + normalize_back(d_in * (1.0 + mod_ref[0, 1:2, :]), normed, inv_std)
    d_h_ref[0] = d_h.astype(d_h_ref.dtype)


def inputs_back(own, other, h, d_mid, mods, dtype):
    latents, tokens, width = h.shape
    rows = row_spec(tokens, width)
    return pl.pallas_call(
        inputs_back_kernel,
        grid=(latents,),
        out_shape=(sized(h.shape, dtype), sized((latents, 2, width), F32)),
        in_specs=[rows, rows, rows, rows, mod_spec(6, width)],
        out_specs=(rows, mod_spec(2, width)),
        compiler_params=params(),
        cost_estimate=cost(0, 10 << 20),
    )(own, other, h, d_mid, mods)


def body(boundary, timestep, label, label_table, ada_weight, qkv_weight, out_weight, up_weight, down_weight):
    on_first = lax.axis_index("section") == 0
    seq = lax.axis_index("seq")
    low, high = seq % 2, seq // 2
    fsdp = lax.axis_index("fsdp")
    n_seq, n_fsdp, n_sec = lax.axis_size("seq"), lax.axis_size("fsdp"), lax.axis_size("section")
    assert n_seq == 4
    place = jnp.stack([low, high, fsdp]).astype(jnp.int32)
    width = boundary.shape[-1]
    tokens_here = boundary.shape[2]
    latents = boundary.shape[1] // 2
    ada, wqkv, wout, wup, wdown = (a[0] for a in (ada_weight, qkv_weight, out_weight, up_weight, down_weight))
    share = wqkv.shape[0]

    def by_core(here, there):
        return jnp.where(low == 0, here, there), jnp.where(low == 0, there, here)

    attn_own, attn_mine = pick_columns((wqkv, wout), (3, 1), place)
    up_own, up_mine = pick_columns((wup,), (n_fsdp,), place)
    sub = wdown.shape[0] // 2
    down_own = lax.dynamic_slice_in_dim(wdown, low * sub, sub, 0)
    down_mine = lax.dynamic_slice_in_dim(wdown, low * sub + high * (sub // 2), sub // 2, 0)

    own = boundary[0]
    stay = lax.dynamic_slice_in_dim(own, high * latents, latents, 0)
    leave = lax.dynamic_slice_in_dim(own, (1 - high) * latents, latents, 0)
    leave = y_swap(after(leave, attn_mine))

    cond = embed_time(timestep, width) + jnp.take(label_table, label, axis=0).astype(F32)
    silu_cond = jax.nn.silu(cond).astype(BF)
    silu_all = gather_back(after(silu_cond, attn_mine, up_mine), "fsdp")
    rest = {}

    def between(k, i, token):
        if (k, i) == (1, 0):
            cols = lax.dynamic_slice_in_dim(together(silu_all, token), fsdp * share, share, 2)
            mine = lax.dynamic_slice_in_dim(cols, high * latents, latents, 1)
            parts = mm(mine.reshape(-1, share), ada).reshape(n_fsdp, latents, -1)
            rest["silu_cols"] = cols.reshape(-1, share)
            rest["mods"] = send_back(parts, "fsdp")
            half = jnp.concatenate([stay, after(leave, parts)], axis=1)
            rest["rows"] = jnp.concatenate(by_core(half, core_swap(half)), axis=1)
            return parts
        if (k, i) == (2, 2):
            mods = jnp.sum(together(rest["mods"], token), axis=0)
            rest["mods"] = mods.reshape(latents, 6, width)
            return mods
        return token

    full_attn, full_up, full_down = whole_weights(
        (attn_own, up_own, down_own), (attn_mine, up_mine, down_mine), place, between
    )
    full_qkv = full_attn
    full_out = join_cores(full_attn, width // 2, place)
    silu_cols, mods, own_rows = rest["silu_cols"], rest["mods"], rest["rows"]

    def cross(rows, step):
        half_tokens = rows.shape[1] // 2
        mine = lax.dynamic_slice_in_dim(rows, low * half_tokens, half_tokens, 1)
        route = [(i, i + step) for i in range(n_sec) if 0 <= i + step < n_sec]
        here = lax.ppermute(mine, "section", route)
        return jnp.concatenate(by_core(here, core_swap(here)), axis=1)

    gate_two = mods[:, 5:6]

    _, att = attend(own_rows, mods, full_qkv, False)
    part, midway = mlp(place, own_rows, mods, att, core_swap(att), full_out, full_up, full_down, False)
    mlp_out = part.astype(F32) + core_swap(part).astype(F32)
    passed = cross((midway + gate_two * mlp_out).astype(BF), 1)

    h = jnp.where(on_first, own_rows, passed)
    qkv, att, attn_in, logs = attend(h, mods, full_qkv, True)
    att_other = core_swap(att)
    part, midway, projected, mlp_in, slope, hidden = mlp(
        place, h, mods, att, att_other, full_out, full_up, full_down, True
    )
    mlp_out = part.astype(F32) + core_swap(part).astype(F32)
    layer_out = midway + gate_two * mlp_out

    back_part, _ = mlp_back(own_rows, mods, slope, full_down, full_up)
    part_two, d_mid, _, _, _ = attend_back(
        place, back_part, core_swap(back_part), own_rows, midway, projected, mods, qkv, logs, full_out, full_qkv
    )
    first_d_h, _ = inputs_back(part_two, core_swap(part_two), h, d_mid, mods, BF)
    incoming = cross(first_d_h, -1)

    def flat(a):
        return a.reshape(-1, a.shape[-1])

    ring = small(n_fsdp)

    def ring_start(blocks):
        return shift(ring_block(blocks, 1), "fsdp", 1)

    def scatter(blocks):
        return lax.psum_scatter(blocks, "fsdp", scatter_dimension=0, tiled=False)

    def y_add(mine, there):
        return (mine.astype(F32) + there.astype(F32)).astype(BF)

    g = jnp.where(on_first, incoming, own_rows)
    d_mlp = (gate_two * g.astype(F32)).astype(BF)
    back_part, d_pre = mlp_back(g, mods, slope, full_down, full_up)
    back_there = core_swap(back_part)
    up_mine, up_other = weight_grad(flat(mlp_in), flat(d_pre), place, True)
    up_there = y_swap(up_other)
    (down,) = weight_grad(flat(hidden), after(flat(d_mlp), up_mine), place, False)
    runs = {}

    def begin(name, blocks):
        runs[name] = (blocks, ring_start(blocks) if ring else None)
        return blocks

    def step(name, back, token):
        blocks, run = runs[name]
        if not ring:
            return scatter(blocks) if back == n_fsdp else blocks
        part = ring_add(blocks, back, after(run, token))
        if back < n_fsdp:
            runs[name] = (blocks, shift(part, "fsdp", 1))
        return part

    begin("down", down)
    part_two, d_mid, d_proj, d_qkv, sums_mid = attend_back(
        place, after(back_part, down), back_there, g, midway, projected, mods, qkv, logs, full_out, full_qkv
    )
    two_there = core_swap(part_two)
    last = step("down", 2, part_two)
    qkv_mine, qkv_other = weight_grad(flat(attn_in), after(flat(d_qkv), last), place, True)
    cols = width // 2
    own_cols = lax.dynamic_slice_in_dim(flat(d_proj), low * cols, cols, 1)
    attended = jnp.concatenate(by_core(flat(att), flat(att_other)), axis=1)
    out_mine, out_other = weight_grad(after(attended, qkv_mine), own_cols, place, True)
    attn_mine = jnp.concatenate([qkv_mine, out_mine], axis=2)
    attn_there = y_swap(jnp.concatenate([qkv_other, out_other], axis=2))
    d_h, sums_in = inputs_back(after(part_two, attn_mine), two_there, h, d_mid, mods, F32)
    last = begin("up", y_add(up_mine, after(up_there, d_h)))
    last = step("down", 3, last)
    last = step("up", 2, last)

    d_gate_two = jnp.sum(g.astype(F32) * mlp_out, axis=1)
    d_mod = jnp.concatenate([part.reshape(latents, -1) for part in (sums_in, sums_mid, d_gate_two)], axis=1)
    d_mine = after(d_mod.astype(BF), last)
    d_there = y_swap(d_mine)
    last = begin("attn", y_add(attn_mine, after(attn_there, d_mine)))
    last = down_part = step("down", 4 if ring else n_fsdp, last)
    down_there = y_swap(down_part)
    last = step("up", 3, last)
    d_there = after(d_there, last)
    d_six = jnp.where(
        high == 0, jnp.concatenate([d_mine, d_there]), jnp.concatenate([d_there, d_mine])
    )
    d_all = gather_back(after(d_six, last), "fsdp")
    last = step("attn", 2, last)
    last = up_part = step("up", 4 if ring else n_fsdp, last)
    up_last, up_core = y_swap(up_part), core_swap(up_part)
    d_all = together(d_all, last).reshape(-1, d_six.shape[1])
    d_silu = mm_nt(d_all, ada).reshape(n_fsdp, 2 * latents, share)
    d_silu = send_back(d_silu, "fsdp")
    last = step("attn", 3, last)
    ada_cols = ada.shape[1] // n_seq
    g_ada = mm_tn(silu_cols, lax.dynamic_slice_in_dim(after(d_all, last), seq * ada_cols, ada_cols, 1))
    last = attn_part = step("attn", 4 if ring else n_fsdp, last)
    attn_last, attn_core = y_swap(attn_part), core_swap(attn_part)

    d_silu = together(d_silu, last)
    ordered = jnp.concatenate([d_silu, d_silu[:-1]])
    d_silu = lax.dynamic_slice_in_dim(ordered, (n_fsdp - fsdp) % n_fsdp, n_fsdp, 0)
    d_silu = d_silu.transpose(1, 0, 2).reshape(2 * latents, width)
    cond_grad = jax.vjp(jax.nn.silu, cond)[1](d_silu)[0]

    down_sum = y_add(down_part, down_there)
    g_down = jnp.concatenate(by_core(down_sum, core_swap(down_sum))).astype(F32)
    g_up = finish((up_part, up_last, up_core, core_swap(up_last)), (n_fsdp,), place)[0]
    g_qkv, g_out = finish((attn_part, attn_last, attn_core, core_swap(attn_last)), (3, 1), place)

    result = jnp.where(on_first, d_h, layer_out)
    blocks = result.reshape(latents, 2, 2, tokens_here, width)
    blocks = lax.dynamic_index_in_dim(blocks, low, 1, keepdims=False)
    keep = blocks[:, 0]
    arrive = after(y_swap(blocks[:, 1].astype(BF)), attn_part).astype(F32)
    end_rows = jnp.where(
        high == 0, jnp.concatenate([keep, arrive], axis=0), jnp.concatenate([arrive, keep], axis=0)
    )
    return (
        end_rows[None],
        cond_grad[None],
        g_ada[None],
        g_qkv[None],
        g_out[None],
        g_up[None],
        g_down[None],
    )


def solution(mesh):
    rows = P("section", "fsdp", "seq", None)
    weight = P("section", "fsdp", None)
    return jax.shard_map(
        body,
        mesh=mesh,
        in_specs=(rows, P("fsdp"), P("fsdp"), P(), weight, weight, weight, weight, weight),
        out_specs=(rows, weight, P("section", "fsdp", "seq"), weight, weight, weight, weight),
        check_vma=False,
    )
```

```python
import math

import jax
import jax.numpy as jnp
from jax import lax
from jax.experimental import pallas as pl
from jax.experimental.pallas import tpu as pltpu
from jax.sharding import PartitionSpec as P

HD = 64
EPS = 1e-06
BF = jnp.bfloat16
F32 = jnp.float32


def dot(a, b, dims):
    return lax.dot_general(a, b, (dims, ((), ())), preferred_element_type=F32)


def mm(a, b):
    return dot(a, b, ((1,), (0,)))


def mm_nt(a, b):
    return dot(a, b, ((1,), (1,)))


def mm_tn(a, b):
    return dot(a, b, ((0,), (0,)))


def after(x, *tokens):
    return lax.optimization_barrier((x,) + tokens)[0]


def core_swap(x):
    return lax.ppermute(x, "seq", [(i, i ^ 1) for i in range(lax.axis_size("seq"))])


def y_swap(x):
    return lax.ppermute(x, "seq", [(i, i ^ 2) for i in range(lax.axis_size("seq"))])


def shift(x, axis, distance):
    n = lax.axis_size(axis)
    return lax.ppermute(x, axis, [(i, (i + distance) % n) for i in range(n)])


def small(n):
    return n == 4


def gather_back(x, axis):
    n = lax.axis_size(axis)
    if not small(n):
        whole = jnp.flip(lax.all_gather(x, axis), 0)
        doubled = jnp.concatenate([whole, whole])
        whole = lax.dynamic_slice_in_dim(doubled, n - 1 - lax.axis_index(axis), n, 0)
        return [whole[k] for k in range(n)]
    return [x] + [shift(x, axis, k) for k in range(1, n)]


def send_back(x, axis):
    n = lax.axis_size(axis)
    if not small(n):
        me = lax.axis_index(axis)
        doubled = jnp.concatenate([x, x])
        whole = jnp.flip(lax.dynamic_slice_in_dim(doubled, (me + 1) % n, n, 0), 0)
        got = lax.all_to_all(whole, axis, split_axis=0, concat_axis=0, tiled=True)
        got = lax.dynamic_slice_in_dim(jnp.concatenate([got, got]), me, n, 0)
        return [got[k] for k in range(n)]
    return [x[0]] + [shift(x[k], axis, n - k) for k in range(1, n)]


def together(pieces, token):
    return jnp.stack(lax.optimization_barrier(tuple(pieces) + (token,))[:-1])


ANY = pl.BlockSpec(memory_space=pl.ANY)
SCALARS = pl.BlockSpec(memory_space=pltpu.SMEM)
VMEM = pl.BlockSpec(memory_space=pltpu.VMEM)


def params(mib=26):
    return pltpu.CompilerParams(vmem_limit_bytes=mib << 20)


def cost(flops, moved):
    return pl.CostEstimate(flops=int(flops), bytes_accessed=int(moved), transcendentals=0)


def sized(shape, dtype):
    return jax.ShapeDtypeStruct(shape, dtype)


def pick_kernel(blocks, place, *refs):
    w_refs, (own_ref, mine_ref) = refs[:-2], refs[-2:]
    at = 0
    for w_ref, count in zip(w_refs, blocks):
        block = w_ref.shape[1] // count // 2
        for b in range(count):
            start = pl.multiple_of((2 * b + place[0]) * block, 128)
            own_ref[:, at : at + block] = w_ref[:, pl.ds(start, block)]
            at += block
    half = mine_ref.shape[0]
    mine_ref[...] = own_ref[pl.ds(pl.multiple_of(place[1] * half, 16), half), :]


def pick_columns(ws, blocks, place):
    rows = ws[0].shape[0]
    half = rows // 2
    sizes = [w.shape[1] // count // 2 for w, count in zip(ws, blocks)]
    if half % 16 or any(size % 128 for size in sizes):
        own = jnp.concatenate(
            [
                lax.dynamic_index_in_dim(w.reshape(rows, count, 2, -1), place[0], 2, keepdims=False).reshape(rows, -1)
                for w, count in zip(ws, blocks)
            ],
            axis=1,
        )
        return own, lax.dynamic_slice_in_dim(own, place[1] * half, half, 0)
    cols = sum(w.shape[1] for w in ws) // 2
    return pl.pallas_call(
        lambda *refs: pick_kernel(blocks, *refs),
        out_shape=(sized((rows, cols), BF), sized((half, cols), BF)),
        in_specs=[SCALARS] + [VMEM] * len(ws),
        out_specs=(VMEM, VMEM),
        compiler_params=params(),
        cost_estimate=cost(0, 8 * rows * cols),
    )(place, *ws)


def assemble_kernel(n, share, place, own_ref, *refs):
    mine_refs, other_refs, out_ref, sems = refs[: n - 1], refs[n - 1 : 2 * n - 2], refs[-2], refs[-1]
    half = share // 2
    me = place[2]

    def rows(start, size):
        return out_ref.at[pl.ds(pl.multiple_of(start, 16), size)]

    copies = [pltpu.make_async_copy(own_ref, rows(me * share, share), sems.at[0])]
    for k in range(1, n):
        base = lax.rem(me - k + n, n) * share
        for j, (ref, part) in enumerate(((mine_refs[k - 1], place[1]), (other_refs[k - 1], 1 - place[1]))):
            copies.append(
                pltpu.make_async_copy(ref, rows(base + part * half, half), sems.at[2 * k - 1 + j])
            )
    for copy in copies:
        copy.start()
    for copy in copies:
        copy.wait()


def assemble(own, mine, other, place):
    n = len(mine) + 1
    share = own.shape[0]
    return pl.pallas_call(
        lambda *refs: assemble_kernel(n, share, *refs),
        out_shape=sized((n * share, own.shape[1]), own.dtype),
        in_specs=[SCALARS] + [ANY] * (2 * n - 1),
        out_specs=ANY,
        scratch_shapes=[pltpu.SemaphoreType.DMA((2 * n - 1,))],
        compiler_params=params(),
        cost_estimate=cost(0, 2 * n * share * own.shape[1] * 2),
    )(place, own, *mine, *other)


def whole_weights(owns, mines, place, between):
    n = lax.axis_size("fsdp")
    if not small(n):
        for at in ((1, 0), (1, 2), (3, 0)):
            between(*at, mines[0])
        whole = []
        for own, mine in zip(owns, mines):
            here = lax.all_gather(mine, "fsdp")
            there = y_swap(here)
            pair = jnp.where(place[1] == 0, jnp.stack([here, there], 1), jnp.stack([there, here], 1))
            whole.append(pair.reshape(n * own.shape[0], own.shape[1]))
        return whole
    runs = [shift(mine, "fsdp", 1) for mine in mines]
    arrived, there = [[] for _ in mines], [[] for _ in mines]
    last, swaps = mines[0], []
    for k in range(1, n):
        for i in range(len(runs)):
            block = after(runs[i], last, *swaps[-2:-1])
            arrived[i].append(block)
            if k < n - 1:
                runs[i] = shift(block, "fsdp", 1)
            swaps.append(y_swap(block))
            there[i].append(swaps[-1])
            last = between(k, i, block)
    return [assemble(*four, place) for four in zip(owns, arrived, there)]


def join_kernel(place, here_ref, there_ref, out_ref):
    cols = there_ref.shape[1]
    here = here_ref[:, here_ref.shape[1] - cols :]
    out_ref[:, pl.ds(pl.multiple_of(place[0] * cols, 128), cols)] = here
    out_ref[:, pl.ds(pl.multiple_of((1 - place[0]) * cols, 128), cols)] = there_ref[...]


def join_cores(here, cols, place):
    rows = here.shape[0]
    there = core_swap(here[:, here.shape[1] - cols :])
    return pl.pallas_call(
        join_kernel,
        out_shape=sized((rows, 2 * cols), here.dtype),
        in_specs=[SCALARS, VMEM, VMEM],
        out_specs=VMEM,
        compiler_params=params(),
        cost_estimate=cost(0, 8 * rows * cols),
    )(place, here, there)


def ring_block(blocks, back):
    n = lax.axis_size("fsdp")
    return lax.dynamic_index_in_dim(blocks, (lax.axis_index("fsdp") + n - back) % n, 0, keepdims=False)


def ring_add(blocks, back, arrived):
    return (ring_block(blocks, back).astype(F32) + arrived.astype(F32)).astype(BF)


def grad_kernel(group, split, place, x_ref, d_ref, *refs):
    out_refs, whole_ref = refs[:-1], refs[-1]
    whole_ref[...] = mm_tn(x_ref[...], d_ref[...])
    size = out_refs[0].shape[1]
    for z in range(out_refs[0].shape[0]):
        for ref, part in zip(out_refs, (place[1], 1 - place[1]) if split else (0,)):
            start = pl.multiple_of(z * group + part * size, 8)
            ref[z] = whole_ref[pl.ds(start, size), :].astype(BF)


def weight_grad(x, d, place, split):
    n = lax.axis_size("fsdp")
    rows, cols = x.shape
    out = d.shape[1]
    group = cols // n
    block = min(cols, 384)
    if group > block or block % group or cols % block or group % 32:
        whole = mm_tn(x, d).astype(BF).reshape(n, 2 if split else 1, -1, out)
        halves = (place[1], 1 - place[1]) if split else (0,)
        return [lax.dynamic_index_in_dim(whole, h, 1, keepdims=False) for h in halves]
    size = group // 2 if split else group
    count = 2 if split else 1
    return pl.pallas_call(
        lambda *refs: grad_kernel(group, split, *refs),
        grid=(cols // block,),
        out_shape=(sized((n, size, out), BF),) * count,
        in_specs=[SCALARS, pl.BlockSpec((rows, block), lambda i: (0, i)), VMEM],
        out_specs=(pl.BlockSpec((block // group, size, out), lambda i: (i, 0, 0)),) * count,
        scratch_shapes=[pltpu.VMEM((block, out), F32)],
        compiler_params=params(),
        cost_estimate=cost(2 * rows * cols * out, 2 * (rows * (cols + out) + cols * out)),
    )(place, x, d)


def finish_kernel(blocks, sizes, place, *refs):
    pieces, out_refs = refs[:4], refs[4:]
    half = pieces[0].shape[0]
    row = [pl.multiple_of(part * half, 8) for part in (place[1], 1 - place[1])]
    for c in range(2):
        core = place[0] if c == 0 else 1 - place[0]
        for r in range(2):
            start = 0
            for out_ref, count, block in zip(out_refs, blocks, sizes):
                for b in range(count):
                    at = pl.multiple_of((2 * b + core) * block, 128)
                    got = pieces[2 * c + r][:, start : start + block].astype(F32)
                    out_ref[pl.ds(row[r], half), pl.ds(at, block)] = got
                    start += block


def finish(pieces, blocks, place):
    half, cols = pieces[0].shape
    sizes = [cols // sum(blocks)] * len(blocks)
    if half % 16 or sizes[0] % 128:
        def order(mine, there):
            return jnp.where(place[1] == 0, jnp.concatenate([mine, there]), jnp.concatenate([there, mine]))

        here, there = (order(*p).reshape(2 * half, sum(blocks), -1) for p in (pieces[:2], pieces[2:]))
        pair = [jnp.where(place[0] == 0, here, there), jnp.where(place[0] == 0, there, here)]
        whole = jnp.stack(pair, 2).astype(F32)
        got, start = [], 0
        for count in blocks:
            got.append(whole[:, start : start + count].reshape(2 * half, -1))
            start += count
        return got
    return pl.pallas_call(
        lambda *refs: finish_kernel(blocks, sizes, *refs),
        out_shape=tuple(sized((2 * half, 2 * count * size), F32) for count, size in zip(blocks, sizes)),
        in_specs=[SCALARS] + [VMEM] * 4,
        out_specs=(VMEM,) * len(blocks),
        compiler_params=params(),
        cost_estimate=cost(0, 24 * half * cols),
    )(place, *pieces)


def embed_time(timestep, width):
    half = width // 2
    frequency = jnp.exp(-math.log(10000.0) * jnp.arange(half, dtype=F32) / half)
    angles = timestep.astype(F32)[:, None] * frequency[None, :]
    return jnp.concatenate([jnp.cos(angles), jnp.sin(angles)], axis=1)


def normalize(v):
    centered = v - jnp.mean(v, axis=-1, keepdims=True)
    inv_std = lax.rsqrt(jnp.mean(centered * centered, axis=-1, keepdims=True) + EPS)
    return centered * inv_std, inv_std


def normalize_back(u, normed, inv_std):
    return inv_std * (
        u
        - jnp.mean(u, axis=-1, keepdims=True)
        - normed * jnp.mean(u * normed, axis=-1, keepdims=True)
    )


ROOT = math.sqrt(2.0 / math.pi)


def gelu(v):
    square = v * v
    t = jnp.tanh(v * (ROOT + (ROOT * 0.044715) * square))
    half = 0.5 * v
    return half + half * t, t, half, square


def gelu_slope(t, half, square):
    inner = ROOT + (3.0 * 0.044715 * ROOT) * square
    return (0.5 + 0.5 * t) + (half * inner) * (1.0 - t * t)


def lanes_of(shape, which):
    lane = lax.broadcasted_iota(jnp.int32, shape, 1)
    return (lane < HD) if which == 0 else (lane >= HD)


def keep_head(pair, which):
    return jnp.where(lanes_of(pair.shape, which), pair, jnp.zeros_like(pair))


def keep_rows(pair, which):
    row = lax.broadcasted_iota(jnp.int32, pair.shape, 0)
    return jnp.where((row < HD) if which == 0 else (row >= HD), pair, jnp.zeros_like(pair))


def attend_kernel(h_ref, mod_ref, w_ref, qkv_ref, att_ref, in_ref=None, log_ref=None):
    h = h_ref[0].astype(F32)
    normed, _ = normalize(h)
    x = (normed * (1.0 + mod_ref[0, 1:2, :]) + mod_ref[0, 0:1, :]).astype(BF)
    if in_ref is not None:
        in_ref[0] = x
    cols = qkv_ref.shape[2] // 3
    for part in range(3):
        qkv_ref[0, :, part * cols : (part + 1) * cols] = mm(
            x, w_ref[:, part * cols : (part + 1) * cols]
        ).astype(BF)
    for pair in range(cols // (2 * HD)):
        at = pair * 2 * HD
        q = qkv_ref[0, :, at : at + 2 * HD] * (1.0 / math.sqrt(HD))
        k = qkv_ref[0, :, cols + at : cols + at + 2 * HD]
        v_t = qkv_ref[0, :, 2 * cols + at : 2 * cols + at + 2 * HD].T
        total = None
        for which in range(2):
            s_t = mm_nt(k, keep_head(q, which))
            top = jnp.max(s_t, axis=0, keepdims=True)
            e = jnp.exp(s_t - top)
            whole = jnp.sum(e, axis=0, keepdims=True)
            if log_ref is not None:
                log_ref[0, 2 * pair + which : 2 * pair + which + 1, :] = top + jnp.log(whole)
            o_t = mm(keep_rows(v_t, which), (e * (1.0 / whole)).astype(BF))
            total = o_t if total is None else total + o_t
        att_ref[0, :, at : at + 2 * HD] = total.astype(BF).T


def row_spec(tokens, width):
    return pl.BlockSpec((1, tokens, width), lambda i: (i, 0, 0))


def mod_spec(parts, width):
    return pl.BlockSpec((1, parts, width), lambda i: (i, 0, 0))


def attend(h, mods, wqkv, keep):
    latents, tokens, width = h.shape
    cols = 3 * width // 2
    outs = [(tokens, cols, BF), (tokens, cols // 3, BF)]
    if keep:
        outs += [(tokens, width, BF), (cols // 3 // HD, tokens, F32)]
    return pl.pallas_call(
        attend_kernel,
        grid=(latents,),
        out_shape=tuple(sized((latents, r, c), t) for r, c, t in outs),
        in_specs=[row_spec(tokens, width), mod_spec(6, width), VMEM],
        out_specs=tuple(row_spec(r, c) for r, c, _ in outs),
        compiler_params=params(),
        cost_estimate=cost(latents * tokens * (2 * width * cols + 8 * tokens * cols), 8 << 20),
    )(h, mods, wqkv)


CHUNK = 512


def mlp_kernel(place, h_ref, mod_ref, own_ref, other_ref, wout_ref, wup_ref, wdown_ref,
               part_ref, midway_ref, proj_ref=None, in_ref=None, slope_ref=None, hidden_ref=None):
    half = own_ref.shape[2]
    low = place[0]
    projected = mm(own_ref[0], wout_ref[pl.ds(pl.multiple_of(low * half, 128), half), :])
    projected += mm(other_ref[0], wout_ref[pl.ds(pl.multiple_of((1 - low) * half, 128), half), :])
    midway = h_ref[0].astype(F32) + mod_ref[0, 2:3, :] * projected
    midway_ref[0] = midway
    normed, _ = normalize(midway)
    x = (normed * (1.0 + mod_ref[0, 4:5, :]) + mod_ref[0, 3:4, :]).astype(BF)
    if proj_ref is not None:
        proj_ref[0] = projected.astype(BF)
        in_ref[0] = x
    total = None
    for at in range(0, wup_ref.shape[1], CHUNK):
        pre = mm(x, wup_ref[:, at : at + CHUNK])
        hidden, *rest = gelu(pre)
        hidden = hidden.astype(BF)
        if slope_ref is not None:
            slope_ref[0, :, at : at + CHUNK] = gelu_slope(*rest).astype(BF)
            hidden_ref[0, :, at : at + CHUNK] = hidden
        part = mm(hidden, wdown_ref[at : at + CHUNK, :])
        total = part if total is None else total + part
    part_ref[0] = total.astype(BF)


def mlp(place, h, mods, own, other, wout, wup, wdown, keep):
    latents, tokens, width = h.shape
    units = wup.shape[1]
    half = own.shape[2]
    outs = [(width, BF), (width, F32)]
    if keep:
        outs += [(width, BF), (width, BF), (units, BF), (units, BF)]
    return pl.pallas_call(
        mlp_kernel,
        grid=(latents,),
        out_shape=tuple(sized((latents, tokens, c), t) for c, t in outs),
        in_specs=[SCALARS, row_spec(tokens, width), mod_spec(6, width), row_spec(tokens, half),
                  row_spec(tokens, half), VMEM, VMEM, VMEM],
        out_specs=tuple(row_spec(tokens, c) for c, _ in outs),
        compiler_params=params(),
        cost_estimate=cost(latents * tokens * 2 * width * (2 * units + width), 16 << 20),
    )(place, h, mods, own, other, wout, wup, wdown)


def mlp_back_kernel(g_ref, mod_ref, slope_ref, wdown_ref, wup_ref, part_ref, d_pre_ref):
    d_mlp = (mod_ref[0, 5:6, :] * g_ref[0].astype(F32)).astype(BF)
    total = None
    for at in range(0, wup_ref.shape[1], CHUNK):
        d_hidden = mm_nt(d_mlp, wdown_ref[at : at + CHUNK, :])
        d_pre = (d_hidden * slope_ref[0, :, at : at + CHUNK].astype(F32)).astype(BF)
        d_pre_ref[0, :, at : at + CHUNK] = d_pre
        part = mm_nt(d_pre, wup_ref[:, at : at + CHUNK])
        total = part if total is None else total + part
    part_ref[0] = total.astype(BF)


def mlp_back(g, mods, slope, wdown, wup):
    latents, tokens, width = g.shape
    units = wup.shape[1]
    return pl.pallas_call(
        mlp_back_kernel,
        grid=(latents,),
        out_shape=(sized((latents, tokens, width), BF), sized((latents, tokens, units), BF)),
        in_specs=[row_spec(tokens, width), mod_spec(6, width), row_spec(tokens, units), VMEM, VMEM],
        out_specs=(row_spec(tokens, width), row_spec(tokens, units)),
        compiler_params=params(),
        cost_estimate=cost(latents * tokens * 4 * width * units, 14 << 20),
    )(g, mods, slope, wdown, wup)


def attend_back_kernel(place, own_ref, other_ref, g_ref, midway_ref, proj_ref, mod_ref, qkv_ref, log_ref,
                       wout_ref, wqkv_ref, part_ref, d_mid_ref, d_proj_ref, d_qkv_ref, sums_ref):
    d_in = own_ref[0].astype(F32) + other_ref[0].astype(F32)
    normed, inv_std = normalize(midway_ref[0])
    sums_ref[0, 1:2, :] = jnp.sum(d_in, axis=0, keepdims=True)
    sums_ref[0, 2:3, :] = jnp.sum(d_in * normed, axis=0, keepdims=True)
    d_mid = g_ref[0].astype(F32) + normalize_back(d_in * (1.0 + mod_ref[0, 4:5, :]), normed, inv_std)
    d_mid_ref[0] = d_mid
    d_proj = (mod_ref[0, 2:3, :] * d_mid).astype(BF)
    d_proj_ref[0] = d_proj
    sums_ref[0, 0:1, :] = jnp.sum(d_mid * proj_ref[0].astype(F32), axis=0, keepdims=True)
    cols = d_qkv_ref.shape[2] // 3
    low = place[0]
    d_att = mm_nt(d_proj, wout_ref[pl.ds(pl.multiple_of(low * cols, 128), cols), :]).astype(BF)
    scale = 1.0 / math.sqrt(HD)
    for pair in range(cols // (2 * HD)):
        at = pair * 2 * HD
        q = qkv_ref[0, :, at : at + 2 * HD] * scale
        k = qkv_ref[0, :, cols + at : cols + at + 2 * HD]
        v = qkv_ref[0, :, 2 * cols + at : 2 * cols + at + 2 * HD]
        k_t = k.T
        d_o = d_att[:, at : at + 2 * HD]
        dq_t = dk = dv = 0.0
        for which in range(2):
            q_one, d_one = keep_head(q, which), keep_head(d_o, which)
            log = log_ref[0, 2 * pair + which : 2 * pair + which + 1, :]
            probs_t = jnp.exp(mm_nt(k, q_one) - log)
            weighted = probs_t * mm_nt(v, d_one)
            delta = jnp.sum(weighted, axis=0, keepdims=True)
            d_s_t = (weighted - probs_t * delta).astype(BF)
            dq_t += mm(keep_rows(k_t, which), d_s_t)
            dk += mm(d_s_t, q_one)
            dv += mm(probs_t.astype(BF), d_one)
        d_qkv_ref[0, :, at : at + 2 * HD] = (dq_t * scale).astype(BF).T
        d_qkv_ref[0, :, cols + at : cols + at + 2 * HD] = dk.astype(BF)
        d_qkv_ref[0, :, 2 * cols + at : 2 * cols + at + 2 * HD] = dv.astype(BF)
    part_ref[0] = mm_nt(d_qkv_ref[0], wqkv_ref[:, : 3 * cols]).astype(BF)


def attend_back(place, own, other, g, midway, projected, mods, qkv, logs, wout, wqkv):
    latents, tokens, width = g.shape
    cols = qkv.shape[2]
    rows = row_spec(tokens, width)
    return pl.pallas_call(
        attend_back_kernel,
        grid=(latents,),
        out_shape=(
            sized(g.shape, BF),
            sized(g.shape, F32),
            sized(g.shape, BF),
            sized((latents, tokens, cols), BF),
            sized((latents, 3, width), F32),
        ),
        in_specs=[SCALARS, rows, rows, rows, rows, rows, mod_spec(6, width), row_spec(tokens, cols),
                  row_spec(logs.shape[1], tokens), VMEM, VMEM],
        out_specs=(rows, rows, rows, row_spec(tokens, cols), mod_spec(3, width)),
        compiler_params=params(),
        cost_estimate=cost(latents * tokens * (2 * width * cols + 20 * tokens * cols), 14 << 20),
    )(place, own, other, g, midway, projected, mods, qkv, logs, wout, wqkv)


def inputs_back_kernel(own_ref, other_ref, h_ref, d_mid_ref, mod_ref, d_h_ref, sums_ref):
    d_in = own_ref[0].astype(F32) + other_ref[0].astype(F32)
    normed, inv_std = normalize(h_ref[0].astype(F32))
    sums_ref[0, 0:1, :] = jnp.sum(d_in, axis=0, keepdims=True)
    sums_ref[0, 1:2, :] = jnp.sum(d_in * normed, axis=0, keepdims=True)
    d_h = d_mid_ref[0] + normalize_back(d_in * (1.0 + mod_ref[0, 1:2, :]), normed, inv_std)
    d_h_ref[0] = d_h.astype(d_h_ref.dtype)


def inputs_back(own, other, h, d_mid, mods, dtype):
    latents, tokens, width = h.shape
    rows = row_spec(tokens, width)
    return pl.pallas_call(
        inputs_back_kernel,
        grid=(latents,),
        out_shape=(sized(h.shape, dtype), sized((latents, 2, width), F32)),
        in_specs=[rows, rows, rows, rows, mod_spec(6, width)],
        out_specs=(rows, mod_spec(2, width)),
        compiler_params=params(),
        cost_estimate=cost(0, 10 << 20),
    )(own, other, h, d_mid, mods)


def body(boundary, timestep, label, label_table, ada_weight, qkv_weight, out_weight, up_weight, down_weight):
    on_first = lax.axis_index("section") == 0
    seq = lax.axis_index("seq")
    low, high = seq % 2, seq // 2
    fsdp = lax.axis_index("fsdp")
    n_seq, n_fsdp, n_sec = lax.axis_size("seq"), lax.axis_size("fsdp"), lax.axis_size("section")
    assert n_seq == 4
    place = jnp.stack([low, high, fsdp]).astype(jnp.int32)
    width = boundary.shape[-1]
    tokens_here = boundary.shape[2]
    latents = boundary.shape[1] // 2
    ada, wqkv, wout, wup, wdown = (a[0] for a in (ada_weight, qkv_weight, out_weight, up_weight, down_weight))
    share = wqkv.shape[0]

    def by_core(here, there):
        return jnp.where(low == 0, here, there), jnp.where(low == 0, there, here)

    attn_own, attn_mine = pick_columns((wqkv, wout), (3, 1), place)
    up_own, up_mine = pick_columns((wup,), (n_fsdp,), place)
    sub = wdown.shape[0] // 2
    down_own = lax.dynamic_slice_in_dim(wdown, low * sub, sub, 0)
    down_mine = lax.dynamic_slice_in_dim(wdown, low * sub + high * (sub // 2), sub // 2, 0)

    own = boundary[0]
    stay = lax.dynamic_slice_in_dim(own, high * latents, latents, 0)
    leave = lax.dynamic_slice_in_dim(own, (1 - high) * latents, latents, 0)
    leave = y_swap(after(leave, attn_mine))

    cond = embed_time(timestep, width) + jnp.take(label_table, label, axis=0).astype(F32)
    silu_cond = jax.nn.silu(cond).astype(BF)
    rest = {}

    def between(k, i, token):
        if (k, i) == (1, 0):
            rest["leave"] = after(leave, token)
            rest["silu"] = gather_back(after(silu_cond, rest["leave"]), "fsdp")
        if (k, i) == (1, 2):
            cols = lax.dynamic_slice_in_dim(together(rest["silu"], token), fsdp * share, share, 2)
            mine = lax.dynamic_slice_in_dim(cols, high * latents, latents, 1)
            parts = mm(mine.reshape(-1, share), ada).reshape(n_fsdp, latents, -1)
            rest["silu_cols"] = cols.reshape(-1, share)
            rest["mods"] = send_back(parts, "fsdp")
            half = jnp.concatenate([stay, rest["leave"]], axis=1)
            rest["rows"] = jnp.concatenate(by_core(half, core_swap(half)), axis=1)
            return parts
        if (k, i) == (3, 0):
            mods = jnp.sum(together(rest["mods"], token), axis=0)
            rest["mods"] = mods.reshape(latents, 6, width)
            return mods
        return token

    full_attn, full_up, full_down = whole_weights(
        (attn_own, up_own, down_own), (attn_mine, up_mine, down_mine), place, between
    )
    full_qkv = full_attn
    full_out = join_cores(full_attn, width // 2, place)
    silu_cols, mods, own_rows = rest["silu_cols"], rest["mods"], rest["rows"]

    def cross(rows, step):
        half_tokens = rows.shape[1] // 2
        mine = lax.dynamic_slice_in_dim(rows, low * half_tokens, half_tokens, 1)
        route = [(i, i + step) for i in range(n_sec) if 0 <= i + step < n_sec]
        here = lax.ppermute(mine, "section", route)
        return jnp.concatenate(by_core(here, core_swap(here)), axis=1)

    gate_two = mods[:, 5:6]

    _, att = attend(own_rows, mods, full_qkv, False)
    part, midway = mlp(place, own_rows, mods, att, core_swap(att), full_out, full_up, full_down, False)
    mlp_out = part.astype(F32) + core_swap(part).astype(F32)
    passed = cross((midway + gate_two * mlp_out).astype(BF), 1)

    h = jnp.where(on_first, own_rows, passed)
    qkv, att, attn_in, logs = attend(h, mods, full_qkv, True)
    att_other = core_swap(att)
    part, midway, projected, mlp_in, slope, hidden = mlp(
        place, h, mods, att, att_other, full_out, full_up, full_down, True
    )
    mlp_out = part.astype(F32) + core_swap(part).astype(F32)
    layer_out = midway + gate_two * mlp_out

    back_part, _ = mlp_back(own_rows, mods, slope, full_down, full_up)
    part_two, d_mid, _, _, _ = attend_back(
        place, back_part, core_swap(back_part), own_rows, midway, projected, mods, qkv, logs, full_out, full_qkv
    )
    first_d_h, _ = inputs_back(part_two, core_swap(part_two), h, d_mid, mods, BF)
    incoming = cross(first_d_h, -1)

    def flat(a):
        return a.reshape(-1, a.shape[-1])

    ring = small(n_fsdp)

    def ring_start(blocks):
        return shift(ring_block(blocks, 1), "fsdp", 1)

    def scatter(blocks):
        return lax.psum_scatter(blocks, "fsdp", scatter_dimension=0, tiled=False)

    def y_add(mine, there):
        return (mine.astype(F32) + there.astype(F32)).astype(BF)

    g = jnp.where(on_first, incoming, own_rows)
    d_mlp = (gate_two * g.astype(F32)).astype(BF)
    back_part, d_pre = mlp_back(g, mods, slope, full_down, full_up)
    back_there = core_swap(back_part)
    up_mine, up_other = weight_grad(flat(mlp_in), flat(d_pre), place, True)
    up_there = y_swap(up_other)
    (down,) = weight_grad(flat(hidden), after(flat(d_mlp), up_mine), place, False)
    runs = {}

    def begin(name, blocks):
        runs[name] = (blocks, ring_start(blocks) if ring else None)
        return blocks

    def step(name, back, token):
        blocks, run = runs[name]
        if not ring:
            return scatter(blocks) if back == n_fsdp else blocks
        part = ring_add(blocks, back, after(run, token))
        if back < n_fsdp:
            runs[name] = (blocks, shift(part, "fsdp", 1))
        return part

    begin("down", down)
    part_two, d_mid, d_proj, d_qkv, sums_mid = attend_back(
        place, after(back_part, down), back_there, g, midway, projected, mods, qkv, logs, full_out, full_qkv
    )
    two_there = core_swap(part_two)
    last = step("down", 2, part_two)
    qkv_mine, qkv_other = weight_grad(flat(attn_in), after(flat(d_qkv), last), place, True)
    cols = width // 2
    own_cols = lax.dynamic_slice_in_dim(flat(d_proj), low * cols, cols, 1)
    attended = jnp.concatenate(by_core(flat(att), flat(att_other)), axis=1)
    out_mine, out_other = weight_grad(after(attended, qkv_mine), own_cols, place, True)
    attn_mine = jnp.concatenate([qkv_mine, out_mine], axis=2)
    attn_there = y_swap(jnp.concatenate([qkv_other, out_other], axis=2))
    d_h, sums_in = inputs_back(after(part_two, attn_mine), two_there, h, d_mid, mods, F32)
    last = begin("up", y_add(up_mine, after(up_there, d_h)))
    last = step("down", 3, last)
    last = step("up", 2, last)

    d_gate_two = jnp.sum(g.astype(F32) * mlp_out, axis=1)
    d_mod = jnp.concatenate([part.reshape(latents, -1) for part in (sums_in, sums_mid, d_gate_two)], axis=1)
    d_mine = after(d_mod.astype(BF), last)
    d_there = y_swap(d_mine)
    last = begin("attn", y_add(attn_mine, after(attn_there, d_mine)))
    last = down_part = step("down", 4 if ring else n_fsdp, last)
    down_there = y_swap(down_part)
    last = step("up", 3, last)
    d_there = after(d_there, last)
    d_six = jnp.where(
        high == 0, jnp.concatenate([d_mine, d_there]), jnp.concatenate([d_there, d_mine])
    )
    d_all = gather_back(after(d_six, last), "fsdp")
    last = step("attn", 2, last)
    last = up_part = step("up", 4 if ring else n_fsdp, last)
    up_last, up_core = y_swap(up_part), core_swap(up_part)
    d_all = together(d_all, last).reshape(-1, d_six.shape[1])
    d_silu = mm_nt(d_all, ada).reshape(n_fsdp, 2 * latents, share)
    d_silu = send_back(d_silu, "fsdp")
    last = step("attn", 3, last)
    ada_cols = ada.shape[1] // n_seq
    g_ada = mm_tn(silu_cols, lax.dynamic_slice_in_dim(after(d_all, last), seq * ada_cols, ada_cols, 1))
    last = attn_part = step("attn", 4 if ring else n_fsdp, last)
    attn_last, attn_core = y_swap(attn_part), core_swap(attn_part)

    d_silu = together(d_silu, last)
    ordered = jnp.concatenate([d_silu, d_silu[:-1]])
    d_silu = lax.dynamic_slice_in_dim(ordered, (n_fsdp - fsdp) % n_fsdp, n_fsdp, 0)
    d_silu = d_silu.transpose(1, 0, 2).reshape(2 * latents, width)
    cond_grad = jax.vjp(jax.nn.silu, cond)[1](d_silu)[0]

    down_sum = y_add(down_part, down_there)
    g_down = jnp.concatenate(by_core(down_sum, core_swap(down_sum))).astype(F32)
    g_up = finish((up_part, up_last, up_core, core_swap(up_last)), (n_fsdp,), place)[0]
    g_qkv, g_out = finish((attn_part, attn_last, attn_core, core_swap(attn_last)), (3, 1), place)

    result = jnp.where(on_first, d_h, layer_out)
    blocks = result.reshape(latents, 2, 2, tokens_here, width)
    blocks = lax.dynamic_index_in_dim(blocks, low, 1, keepdims=False)
    keep = blocks[:, 0]
    arrive = after(y_swap(blocks[:, 1].astype(BF)), attn_part).astype(F32)
    end_rows = jnp.where(
        high == 0, jnp.concatenate([keep, arrive], axis=0), jnp.concatenate([arrive, keep], axis=0)
    )
    return (
        end_rows[None],
        cond_grad[None],
        g_ada[None],
        g_qkv[None],
        g_out[None],
        g_up[None],
        g_down[None],
    )


def solution(mesh):
    rows = P("section", "fsdp", "seq", None)
    weight = P("section", "fsdp", None)
    return jax.shard_map(
        body,
        mesh=mesh,
        in_specs=(rows, P("fsdp"), P("fsdp"), P(), weight, weight, weight, weight, weight),
        out_specs=(rows, weight, P("section", "fsdp", "seq"), weight, weight, weight, weight),
        check_vma=False,
    )
```

```python
import math

import jax
import jax.numpy as jnp
from jax import lax
from jax.experimental import pallas as pl
from jax.experimental.pallas import tpu as pltpu
from jax.sharding import PartitionSpec as P

HD = 64
EPS = 1e-06
BF = jnp.bfloat16
F32 = jnp.float32


def dot(a, b, dims):
    return lax.dot_general(a, b, (dims, ((), ())), preferred_element_type=F32)


def mm(a, b):
    return dot(a, b, ((1,), (0,)))


def mm_nt(a, b):
    return dot(a, b, ((1,), (1,)))


def mm_tn(a, b):
    return dot(a, b, ((0,), (0,)))


def after(x, *tokens):
    return lax.optimization_barrier((x,) + tokens)[0]


def core_swap(x):
    return lax.ppermute(x, "seq", [(i, i ^ 1) for i in range(lax.axis_size("seq"))])


def y_swap(x):
    return lax.ppermute(x, "seq", [(i, i ^ 2) for i in range(lax.axis_size("seq"))])


def shift(x, axis, distance):
    n = lax.axis_size(axis)
    return lax.ppermute(x, axis, [(i, (i + distance) % n) for i in range(n)])


def small(n):
    return n == 4


def gather_back(x, axis):
    n = lax.axis_size(axis)
    if not small(n):
        whole = jnp.flip(lax.all_gather(x, axis), 0)
        doubled = jnp.concatenate([whole, whole])
        whole = lax.dynamic_slice_in_dim(doubled, n - 1 - lax.axis_index(axis), n, 0)
        return [whole[k] for k in range(n)]
    return [x] + [shift(x, axis, k) for k in range(1, n)]


def send_back(x, axis):
    n = lax.axis_size(axis)
    if not small(n):
        me = lax.axis_index(axis)
        doubled = jnp.concatenate([x, x])
        whole = jnp.flip(lax.dynamic_slice_in_dim(doubled, (me + 1) % n, n, 0), 0)
        got = lax.all_to_all(whole, axis, split_axis=0, concat_axis=0, tiled=True)
        got = lax.dynamic_slice_in_dim(jnp.concatenate([got, got]), me, n, 0)
        return [got[k] for k in range(n)]
    return [x[0]] + [shift(x[k], axis, n - k) for k in range(1, n)]


def together(pieces, token):
    return jnp.stack(lax.optimization_barrier(tuple(pieces) + (token,))[:-1])


ANY = pl.BlockSpec(memory_space=pl.ANY)
SCALARS = pl.BlockSpec(memory_space=pltpu.SMEM)
VMEM = pl.BlockSpec(memory_space=pltpu.VMEM)


def params(mib=26):
    return pltpu.CompilerParams(vmem_limit_bytes=mib << 20)


def cost(flops, moved):
    return pl.CostEstimate(flops=int(flops), bytes_accessed=int(moved), transcendentals=0)


def sized(shape, dtype):
    return jax.ShapeDtypeStruct(shape, dtype)


def pick_kernel(blocks, place, *refs):
    w_refs, (own_ref, mine_ref) = refs[:-2], refs[-2:]
    at = 0
    for w_ref, count in zip(w_refs, blocks):
        block = w_ref.shape[1] // count // 2
        for b in range(count):
            start = pl.multiple_of((2 * b + place[0]) * block, 128)
            own_ref[:, at : at + block] = w_ref[:, pl.ds(start, block)]
            at += block
    half = mine_ref.shape[0]
    mine_ref[...] = own_ref[pl.ds(pl.multiple_of(place[1] * half, 16), half), :]


def pick_columns(ws, blocks, place):
    rows = ws[0].shape[0]
    half = rows // 2
    sizes = [w.shape[1] // count // 2 for w, count in zip(ws, blocks)]
    if half % 16 or any(size % 128 for size in sizes):
        own = jnp.concatenate(
            [
                lax.dynamic_index_in_dim(w.reshape(rows, count, 2, -1), place[0], 2, keepdims=False).reshape(rows, -1)
                for w, count in zip(ws, blocks)
            ],
            axis=1,
        )
        return own, lax.dynamic_slice_in_dim(own, place[1] * half, half, 0)
    cols = sum(w.shape[1] for w in ws) // 2
    return pl.pallas_call(
        lambda *refs: pick_kernel(blocks, *refs),
        out_shape=(sized((rows, cols), BF), sized((half, cols), BF)),
        in_specs=[SCALARS] + [VMEM] * len(ws),
        out_specs=(VMEM, VMEM),
        compiler_params=params(),
        cost_estimate=cost(0, 8 * rows * cols),
    )(place, *ws)


def assemble_kernel(n, share, place, own_ref, *refs):
    mine_refs, other_refs, out_ref, sems = refs[: n - 1], refs[n - 1 : 2 * n - 2], refs[-2], refs[-1]
    half = share // 2
    me = place[2]

    def rows(start, size):
        return out_ref.at[pl.ds(pl.multiple_of(start, 16), size)]

    copies = [pltpu.make_async_copy(own_ref, rows(me * share, share), sems.at[0])]
    for k in range(1, n):
        base = lax.rem(me - k + n, n) * share
        for j, (ref, part) in enumerate(((mine_refs[k - 1], place[1]), (other_refs[k - 1], 1 - place[1]))):
            copies.append(
                pltpu.make_async_copy(ref, rows(base + part * half, half), sems.at[2 * k - 1 + j])
            )
    for copy in copies:
        copy.start()
    for copy in copies:
        copy.wait()


def assemble(own, mine, other, place):
    n = len(mine) + 1
    share = own.shape[0]
    return pl.pallas_call(
        lambda *refs: assemble_kernel(n, share, *refs),
        out_shape=sized((n * share, own.shape[1]), own.dtype),
        in_specs=[SCALARS] + [ANY] * (2 * n - 1),
        out_specs=ANY,
        scratch_shapes=[pltpu.SemaphoreType.DMA((2 * n - 1,))],
        compiler_params=params(),
        cost_estimate=cost(0, 2 * n * share * own.shape[1] * 2),
    )(place, own, *mine, *other)


def whole_weights(owns, mines, place, between):
    n = lax.axis_size("fsdp")
    if not small(n):
        for at in ((1, 0), (1, 2), (3, 0)):
            between(*at, mines[0])
        whole = []
        for own, mine in zip(owns, mines):
            here = lax.all_gather(mine, "fsdp")
            there = y_swap(here)
            pair = jnp.where(place[1] == 0, jnp.stack([here, there], 1), jnp.stack([there, here], 1))
            whole.append(pair.reshape(n * own.shape[0], own.shape[1]))
        return whole
    runs = [shift(mine, "fsdp", 1) for mine in mines]
    arrived, there = [[] for _ in mines], [[] for _ in mines]
    last, swaps = mines[0], []
    for k in range(1, n):
        for i in range(len(runs)):
            block = after(runs[i], last, *swaps[-2:-1])
            arrived[i].append(block)
            if k < n - 1:
                runs[i] = shift(block, "fsdp", 1)
            swaps.append(y_swap(block))
            there[i].append(swaps[-1])
            last = between(k, i, block)
    return [assemble(*four, place) for four in zip(owns, arrived, there)]


def join_kernel(place, here_ref, there_ref, out_ref):
    cols = there_ref.shape[1]
    here = here_ref[:, here_ref.shape[1] - cols :]
    out_ref[:, pl.ds(pl.multiple_of(place[0] * cols, 128), cols)] = here
    out_ref[:, pl.ds(pl.multiple_of((1 - place[0]) * cols, 128), cols)] = there_ref[...]


def join_cores(here, cols, place):
    rows = here.shape[0]
    there = core_swap(here[:, here.shape[1] - cols :])
    return pl.pallas_call(
        join_kernel,
        out_shape=sized((rows, 2 * cols), here.dtype),
        in_specs=[SCALARS, VMEM, VMEM],
        out_specs=VMEM,
        compiler_params=params(),
        cost_estimate=cost(0, 8 * rows * cols),
    )(place, here, there)


def ring_block(blocks, back):
    n = lax.axis_size("fsdp")
    return lax.dynamic_index_in_dim(blocks, (lax.axis_index("fsdp") + n - back) % n, 0, keepdims=False)


def ring_add(blocks, back, arrived):
    return (ring_block(blocks, back).astype(F32) + arrived.astype(F32)).astype(BF)


def grad_kernel(group, split, place, x_ref, d_ref, *refs):
    out_refs, whole_ref = refs[:-1], refs[-1]
    whole_ref[...] = mm_tn(x_ref[...], d_ref[...])
    size = out_refs[0].shape[1]
    for z in range(out_refs[0].shape[0]):
        for ref, part in zip(out_refs, (place[1], 1 - place[1]) if split else (0,)):
            start = pl.multiple_of(z * group + part * size, 8)
            ref[z] = whole_ref[pl.ds(start, size), :].astype(BF)


def weight_grad(x, d, place, split):
    n = lax.axis_size("fsdp")
    rows, cols = x.shape
    out = d.shape[1]
    group = cols // n
    block = min(cols, 384)
    if group > block or block % group or cols % block or group % 32:
        whole = mm_tn(x, d).astype(BF).reshape(n, 2 if split else 1, -1, out)
        halves = (place[1], 1 - place[1]) if split else (0,)
        return [lax.dynamic_index_in_dim(whole, h, 1, keepdims=False) for h in halves]
    size = group // 2 if split else group
    count = 2 if split else 1
    return pl.pallas_call(
        lambda *refs: grad_kernel(group, split, *refs),
        grid=(cols // block,),
        out_shape=(sized((n, size, out), BF),) * count,
        in_specs=[SCALARS, pl.BlockSpec((rows, block), lambda i: (0, i)), VMEM],
        out_specs=(pl.BlockSpec((block // group, size, out), lambda i: (i, 0, 0)),) * count,
        scratch_shapes=[pltpu.VMEM((block, out), F32)],
        compiler_params=params(),
        cost_estimate=cost(2 * rows * cols * out, 2 * (rows * (cols + out) + cols * out)),
    )(place, x, d)


def finish_kernel(blocks, sizes, place, *refs):
    pieces, out_refs = refs[:4], refs[4:]
    half = pieces[0].shape[0]
    row = [pl.multiple_of(part * half, 8) for part in (place[1], 1 - place[1])]
    for c in range(2):
        core = place[0] if c == 0 else 1 - place[0]
        for r in range(2):
            start = 0
            for out_ref, count, block in zip(out_refs, blocks, sizes):
                for b in range(count):
                    at = pl.multiple_of((2 * b + core) * block, 128)
                    got = pieces[2 * c + r][:, start : start + block].astype(F32)
                    out_ref[pl.ds(row[r], half), pl.ds(at, block)] = got
                    start += block


def finish(pieces, blocks, place):
    half, cols = pieces[0].shape
    sizes = [cols // sum(blocks)] * len(blocks)
    if half % 16 or sizes[0] % 128:
        def order(mine, there):
            return jnp.where(place[1] == 0, jnp.concatenate([mine, there]), jnp.concatenate([there, mine]))

        here, there = (order(*p).reshape(2 * half, sum(blocks), -1) for p in (pieces[:2], pieces[2:]))
        pair = [jnp.where(place[0] == 0, here, there), jnp.where(place[0] == 0, there, here)]
        whole = jnp.stack(pair, 2).astype(F32)
        got, start = [], 0
        for count in blocks:
            got.append(whole[:, start : start + count].reshape(2 * half, -1))
            start += count
        return got
    return pl.pallas_call(
        lambda *refs: finish_kernel(blocks, sizes, *refs),
        out_shape=tuple(sized((2 * half, 2 * count * size), F32) for count, size in zip(blocks, sizes)),
        in_specs=[SCALARS] + [VMEM] * 4,
        out_specs=(VMEM,) * len(blocks),
        compiler_params=params(),
        cost_estimate=cost(0, 24 * half * cols),
    )(place, *pieces)


def embed_time(timestep, width):
    half = width // 2
    frequency = jnp.exp(-math.log(10000.0) * jnp.arange(half, dtype=F32) / half)
    angles = timestep.astype(F32)[:, None] * frequency[None, :]
    return jnp.concatenate([jnp.cos(angles), jnp.sin(angles)], axis=1)


def normalize(v):
    centered = v - jnp.mean(v, axis=-1, keepdims=True)
    inv_std = lax.rsqrt(jnp.mean(centered * centered, axis=-1, keepdims=True) + EPS)
    return centered * inv_std, inv_std


def normalize_back(u, normed, inv_std):
    return inv_std * (
        u
        - jnp.mean(u, axis=-1, keepdims=True)
        - normed * jnp.mean(u * normed, axis=-1, keepdims=True)
    )


ROOT = math.sqrt(2.0 / math.pi)


def gelu(v):
    square = v * v
    t = jnp.tanh(v * (ROOT + (ROOT * 0.044715) * square))
    half = 0.5 * v
    return half + half * t, t, half, square


def gelu_slope(t, half, square):
    inner = ROOT + (3.0 * 0.044715 * ROOT) * square
    return (0.5 + 0.5 * t) + (half * inner) * (1.0 - t * t)


def lanes_of(shape, which):
    lane = lax.broadcasted_iota(jnp.int32, shape, 1)
    return (lane < HD) if which == 0 else (lane >= HD)


def keep_head(pair, which):
    return jnp.where(lanes_of(pair.shape, which), pair, jnp.zeros_like(pair))


def keep_rows(pair, which):
    row = lax.broadcasted_iota(jnp.int32, pair.shape, 0)
    return jnp.where((row < HD) if which == 0 else (row >= HD), pair, jnp.zeros_like(pair))


def attend_kernel(h_ref, mod_ref, w_ref, qkv_ref, att_ref, in_ref=None, log_ref=None):
    h = h_ref[0].astype(F32)
    normed, _ = normalize(h)
    x = (normed * (1.0 + mod_ref[0, 1:2, :]) + mod_ref[0, 0:1, :]).astype(BF)
    if in_ref is not None:
        in_ref[0] = x
    cols = qkv_ref.shape[2] // 3
    for part in range(3):
        qkv_ref[0, :, part * cols : (part + 1) * cols] = mm(
            x, w_ref[:, part * cols : (part + 1) * cols]
        ).astype(BF)
    for pair in range(cols // (2 * HD)):
        at = pair * 2 * HD
        q = qkv_ref[0, :, at : at + 2 * HD] * (1.0 / math.sqrt(HD))
        k = qkv_ref[0, :, cols + at : cols + at + 2 * HD]
        v_t = qkv_ref[0, :, 2 * cols + at : 2 * cols + at + 2 * HD].T
        total = None
        for which in range(2):
            s_t = mm_nt(k, keep_head(q, which))
            top = jnp.max(s_t, axis=0, keepdims=True)
            e = jnp.exp(s_t - top)
            whole = jnp.sum(e, axis=0, keepdims=True)
            if log_ref is not None:
                log_ref[0, 2 * pair + which : 2 * pair + which + 1, :] = top + jnp.log(whole)
            o_t = mm(keep_rows(v_t, which), (e * (1.0 / whole)).astype(BF))
            total = o_t if total is None else total + o_t
        att_ref[0, :, at : at + 2 * HD] = total.astype(BF).T


def row_spec(tokens, width):
    return pl.BlockSpec((1, tokens, width), lambda i: (i, 0, 0))


def mod_spec(parts, width):
    return pl.BlockSpec((1, parts, width), lambda i: (i, 0, 0))


def attend(h, mods, wqkv, keep):
    latents, tokens, width = h.shape
    cols = 3 * width // 2
    outs = [(tokens, cols, BF), (tokens, cols // 3, BF)]
    if keep:
        outs += [(tokens, width, BF), (cols // 3 // HD, tokens, F32)]
    return pl.pallas_call(
        attend_kernel,
        grid=(latents,),
        out_shape=tuple(sized((latents, r, c), t) for r, c, t in outs),
        in_specs=[row_spec(tokens, width), mod_spec(6, width), VMEM],
        out_specs=tuple(row_spec(r, c) for r, c, _ in outs),
        compiler_params=params(),
        cost_estimate=cost(latents * tokens * (2 * width * cols + 8 * tokens * cols), 8 << 20),
    )(h, mods, wqkv)


CHUNK = 768


def mlp_kernel(place, h_ref, mod_ref, own_ref, other_ref, wout_ref, wup_ref, wdown_ref,
               part_ref, midway_ref, proj_ref=None, in_ref=None, slope_ref=None, hidden_ref=None):
    half = own_ref.shape[2]
    low = place[0]
    projected = mm(own_ref[0], wout_ref[pl.ds(pl.multiple_of(low * half, 128), half), :])
    projected += mm(other_ref[0], wout_ref[pl.ds(pl.multiple_of((1 - low) * half, 128), half), :])
    midway = h_ref[0].astype(F32) + mod_ref[0, 2:3, :] * projected
    midway_ref[0] = midway
    normed, _ = normalize(midway)
    x = (normed * (1.0 + mod_ref[0, 4:5, :]) + mod_ref[0, 3:4, :]).astype(BF)
    if proj_ref is not None:
        proj_ref[0] = projected.astype(BF)
        in_ref[0] = x
    total = None
    for at in range(0, wup_ref.shape[1], CHUNK):
        pre = mm(x, wup_ref[:, at : at + CHUNK])
        hidden, *rest = gelu(pre)
        hidden = hidden.astype(BF)
        if slope_ref is not None:
            slope_ref[0, :, at : at + CHUNK] = gelu_slope(*rest).astype(BF)
            hidden_ref[0, :, at : at + CHUNK] = hidden
        part = mm(hidden, wdown_ref[at : at + CHUNK, :])
        total = part if total is None else total + part
    part_ref[0] = total.astype(BF)


def mlp(place, h, mods, own, other, wout, wup, wdown, keep):
    latents, tokens, width = h.shape
    units = wup.shape[1]
    half = own.shape[2]
    outs = [(width, BF), (width, F32)]
    if keep:
        outs += [(width, BF), (width, BF), (units, BF), (units, BF)]
    return pl.pallas_call(
        mlp_kernel,
        grid=(latents,),
        out_shape=tuple(sized((latents, tokens, c), t) for c, t in outs),
        in_specs=[SCALARS, row_spec(tokens, width), mod_spec(6, width), row_spec(tokens, half),
                  row_spec(tokens, half), VMEM, VMEM, VMEM],
        out_specs=tuple(row_spec(tokens, c) for c, _ in outs),
        compiler_params=params(),
        cost_estimate=cost(latents * tokens * 2 * width * (2 * units + width), 16 << 20),
    )(place, h, mods, own, other, wout, wup, wdown)


def mlp_back_kernel(g_ref, mod_ref, slope_ref, wdown_ref, wup_ref, part_ref, d_pre_ref):
    d_mlp = (mod_ref[0, 5:6, :] * g_ref[0].astype(F32)).astype(BF)
    total = None
    for at in range(0, wup_ref.shape[1], CHUNK):
        d_hidden = mm_nt(d_mlp, wdown_ref[at : at + CHUNK, :])
        d_pre = (d_hidden * slope_ref[0, :, at : at + CHUNK].astype(F32)).astype(BF)
        d_pre_ref[0, :, at : at + CHUNK] = d_pre
        part = mm_nt(d_pre, wup_ref[:, at : at + CHUNK])
        total = part if total is None else total + part
    part_ref[0] = total.astype(BF)


def mlp_back(g, mods, slope, wdown, wup):
    latents, tokens, width = g.shape
    units = wup.shape[1]
    return pl.pallas_call(
        mlp_back_kernel,
        grid=(latents,),
        out_shape=(sized((latents, tokens, width), BF), sized((latents, tokens, units), BF)),
        in_specs=[row_spec(tokens, width), mod_spec(6, width), row_spec(tokens, units), VMEM, VMEM],
        out_specs=(row_spec(tokens, width), row_spec(tokens, units)),
        compiler_params=params(),
        cost_estimate=cost(latents * tokens * 4 * width * units, 14 << 20),
    )(g, mods, slope, wdown, wup)


def attend_back_kernel(place, own_ref, other_ref, g_ref, midway_ref, proj_ref, mod_ref, qkv_ref, log_ref,
                       wout_ref, wqkv_ref, part_ref, d_mid_ref, d_proj_ref, d_qkv_ref, sums_ref):
    d_in = own_ref[0].astype(F32) + other_ref[0].astype(F32)
    normed, inv_std = normalize(midway_ref[0])
    sums_ref[0, 1:2, :] = jnp.sum(d_in, axis=0, keepdims=True)
    sums_ref[0, 2:3, :] = jnp.sum(d_in * normed, axis=0, keepdims=True)
    d_mid = g_ref[0].astype(F32) + normalize_back(d_in * (1.0 + mod_ref[0, 4:5, :]), normed, inv_std)
    d_mid_ref[0] = d_mid
    d_proj = (mod_ref[0, 2:3, :] * d_mid).astype(BF)
    d_proj_ref[0] = d_proj
    sums_ref[0, 0:1, :] = jnp.sum(d_mid * proj_ref[0].astype(F32), axis=0, keepdims=True)
    cols = d_qkv_ref.shape[2] // 3
    low = place[0]
    d_att = mm_nt(d_proj, wout_ref[pl.ds(pl.multiple_of(low * cols, 128), cols), :]).astype(BF)
    scale = 1.0 / math.sqrt(HD)
    for pair in range(cols // (2 * HD)):
        at = pair * 2 * HD
        q = qkv_ref[0, :, at : at + 2 * HD] * scale
        k = qkv_ref[0, :, cols + at : cols + at + 2 * HD]
        v = qkv_ref[0, :, 2 * cols + at : 2 * cols + at + 2 * HD]
        k_t = k.T
        d_o = d_att[:, at : at + 2 * HD]
        dq_t = dk = dv = 0.0
        for which in range(2):
            q_one, d_one = keep_head(q, which), keep_head(d_o, which)
            log = log_ref[0, 2 * pair + which : 2 * pair + which + 1, :]
            probs_t = jnp.exp(mm_nt(k, q_one) - log)
            weighted = probs_t * mm_nt(v, d_one)
            delta = jnp.sum(weighted, axis=0, keepdims=True)
            d_s_t = (weighted - probs_t * delta).astype(BF)
            dq_t += mm(keep_rows(k_t, which), d_s_t)
            dk += mm(d_s_t, q_one)
            dv += mm(probs_t.astype(BF), d_one)
        d_qkv_ref[0, :, at : at + 2 * HD] = (dq_t * scale).astype(BF).T
        d_qkv_ref[0, :, cols + at : cols + at + 2 * HD] = dk.astype(BF)
        d_qkv_ref[0, :, 2 * cols + at : 2 * cols + at + 2 * HD] = dv.astype(BF)
    part_ref[0] = mm_nt(d_qkv_ref[0], wqkv_ref[:, : 3 * cols]).astype(BF)


def attend_back(place, own, other, g, midway, projected, mods, qkv, logs, wout, wqkv):
    latents, tokens, width = g.shape
    cols = qkv.shape[2]
    rows = row_spec(tokens, width)
    return pl.pallas_call(
        attend_back_kernel,
        grid=(latents,),
        out_shape=(
            sized(g.shape, BF),
            sized(g.shape, F32),
            sized(g.shape, BF),
            sized((latents, tokens, cols), BF),
            sized((latents, 3, width), F32),
        ),
        in_specs=[SCALARS, rows, rows, rows, rows, rows, mod_spec(6, width), row_spec(tokens, cols),
                  row_spec(logs.shape[1], tokens), VMEM, VMEM],
        out_specs=(rows, rows, rows, row_spec(tokens, cols), mod_spec(3, width)),
        compiler_params=params(),
        cost_estimate=cost(latents * tokens * (2 * width * cols + 20 * tokens * cols), 14 << 20),
    )(place, own, other, g, midway, projected, mods, qkv, logs, wout, wqkv)


def inputs_back_kernel(own_ref, other_ref, h_ref, d_mid_ref, mod_ref, d_h_ref, sums_ref):
    d_in = own_ref[0].astype(F32) + other_ref[0].astype(F32)
    normed, inv_std = normalize(h_ref[0].astype(F32))
    sums_ref[0, 0:1, :] = jnp.sum(d_in, axis=0, keepdims=True)
    sums_ref[0, 1:2, :] = jnp.sum(d_in * normed, axis=0, keepdims=True)
    d_h = d_mid_ref[0] + normalize_back(d_in * (1.0 + mod_ref[0, 1:2, :]), normed, inv_std)
    d_h_ref[0] = d_h.astype(d_h_ref.dtype)


def inputs_back(own, other, h, d_mid, mods, dtype):
    latents, tokens, width = h.shape
    rows = row_spec(tokens, width)
    return pl.pallas_call(
        inputs_back_kernel,
        grid=(latents,),
        out_shape=(sized(h.shape, dtype), sized((latents, 2, width), F32)),
        in_specs=[rows, rows, rows, rows, mod_spec(6, width)],
        out_specs=(rows, mod_spec(2, width)),
        compiler_params=params(),
        cost_estimate=cost(0, 10 << 20),
    )(own, other, h, d_mid, mods)


def body(boundary, timestep, label, label_table, ada_weight, qkv_weight, out_weight, up_weight, down_weight):
    on_first = lax.axis_index("section") == 0
    seq = lax.axis_index("seq")
    low, high = seq % 2, seq // 2
    fsdp = lax.axis_index("fsdp")
    n_seq, n_fsdp, n_sec = lax.axis_size("seq"), lax.axis_size("fsdp"), lax.axis_size("section")
    assert n_seq == 4
    place = jnp.stack([low, high, fsdp]).astype(jnp.int32)
    width = boundary.shape[-1]
    tokens_here = boundary.shape[2]
    latents = boundary.shape[1] // 2
    ada, wqkv, wout, wup, wdown = (a[0] for a in (ada_weight, qkv_weight, out_weight, up_weight, down_weight))
    share = wqkv.shape[0]

    def by_core(here, there):
        return jnp.where(low == 0, here, there), jnp.where(low == 0, there, here)

    attn_own, attn_mine = pick_columns((wqkv, wout), (3, 1), place)
    up_own, up_mine = pick_columns((wup,), (n_fsdp,), place)
    sub = wdown.shape[0] // 2
    down_own = lax.dynamic_slice_in_dim(wdown, low * sub, sub, 0)
    down_mine = lax.dynamic_slice_in_dim(wdown, low * sub + high * (sub // 2), sub // 2, 0)

    own = boundary[0]
    stay = lax.dynamic_slice_in_dim(own, high * latents, latents, 0)
    leave = lax.dynamic_slice_in_dim(own, (1 - high) * latents, latents, 0)
    leave = y_swap(after(leave, attn_mine))

    cond = embed_time(timestep, width) + jnp.take(label_table, label, axis=0).astype(F32)
    silu_cond = jax.nn.silu(cond).astype(BF)
    rest = {}

    def between(k, i, token):
        if (k, i) == (1, 0):
            rest["leave"] = after(leave, token)
            rest["silu"] = gather_back(after(silu_cond, rest["leave"]), "fsdp")
        if (k, i) == (1, 2):
            cols = lax.dynamic_slice_in_dim(together(rest["silu"], token), fsdp * share, share, 2)
            mine = lax.dynamic_slice_in_dim(cols, high * latents, latents, 1)
            parts = mm(mine.reshape(-1, share), ada).reshape(n_fsdp, latents, -1)
            rest["silu_cols"] = cols.reshape(-1, share)
            rest["mods"] = send_back(parts, "fsdp")
            half = jnp.concatenate([stay, rest["leave"]], axis=1)
            rest["rows"] = jnp.concatenate(by_core(half, core_swap(half)), axis=1)
            return parts
        if (k, i) == (3, 0):
            mods = jnp.sum(together(rest["mods"], token), axis=0)
            rest["mods"] = mods.reshape(latents, 6, width)
            return mods
        return token

    full_attn, full_up, full_down = whole_weights(
        (attn_own, up_own, down_own), (attn_mine, up_mine, down_mine), place, between
    )
    full_qkv = full_attn
    full_out = join_cores(full_attn, width // 2, place)
    silu_cols, mods, own_rows = rest["silu_cols"], rest["mods"], rest["rows"]

    def cross(rows, step):
        half_tokens = rows.shape[1] // 2
        mine = lax.dynamic_slice_in_dim(rows, low * half_tokens, half_tokens, 1)
        route = [(i, i + step) for i in range(n_sec) if 0 <= i + step < n_sec]
        here = lax.ppermute(mine, "section", route)
        return jnp.concatenate(by_core(here, core_swap(here)), axis=1)

    gate_two = mods[:, 5:6]

    _, att = attend(own_rows, mods, full_qkv, False)
    part, midway = mlp(place, own_rows, mods, att, core_swap(att), full_out, full_up, full_down, False)
    mlp_out = part.astype(F32) + core_swap(part).astype(F32)
    passed = cross((midway + gate_two * mlp_out).astype(BF), 1)

    h = jnp.where(on_first, own_rows, passed)
    qkv, att, attn_in, logs = attend(h, mods, full_qkv, True)
    att_other = core_swap(att)
    part, midway, projected, mlp_in, slope, hidden = mlp(
        place, h, mods, att, att_other, full_out, full_up, full_down, True
    )
    mlp_out = part.astype(F32) + core_swap(part).astype(F32)
    layer_out = midway + gate_two * mlp_out

    back_part, _ = mlp_back(own_rows, mods, slope, full_down, full_up)
    part_two, d_mid, _, _, _ = attend_back(
        place, back_part, core_swap(back_part), own_rows, midway, projected, mods, qkv, logs, full_out, full_qkv
    )
    first_d_h, _ = inputs_back(part_two, core_swap(part_two), h, d_mid, mods, BF)
    incoming = cross(first_d_h, -1)

    def flat(a):
        return a.reshape(-1, a.shape[-1])

    ring = small(n_fsdp)

    def ring_start(blocks):
        return shift(ring_block(blocks, 1), "fsdp", 1)

    def scatter(blocks):
        return lax.psum_scatter(blocks, "fsdp", scatter_dimension=0, tiled=False)

    def y_add(mine, there):
        return (mine.astype(F32) + there.astype(F32)).astype(BF)

    g = jnp.where(on_first, incoming, own_rows)
    d_mlp = (gate_two * g.astype(F32)).astype(BF)
    back_part, d_pre = mlp_back(g, mods, slope, full_down, full_up)
    back_there = core_swap(back_part)
    up_mine, up_other = weight_grad(flat(mlp_in), flat(d_pre), place, True)
    up_there = y_swap(up_other)
    (down,) = weight_grad(flat(hidden), after(flat(d_mlp), up_mine), place, False)
    runs = {}

    def begin(name, blocks):
        runs[name] = (blocks, ring_start(blocks) if ring else None)
        return blocks

    def step(name, back, token):
        blocks, run = runs[name]
        if not ring:
            return scatter(blocks) if back == n_fsdp else blocks
        part = ring_add(blocks, back, after(run, token))
        if back < n_fsdp:
            runs[name] = (blocks, shift(part, "fsdp", 1))
        return part

    begin("down", down)
    part_two, d_mid, d_proj, d_qkv, sums_mid = attend_back(
        place, after(back_part, down), back_there, g, midway, projected, mods, qkv, logs, full_out, full_qkv
    )
    two_there = core_swap(part_two)
    last = step("down", 2, part_two)
    qkv_mine, qkv_other = weight_grad(flat(attn_in), after(flat(d_qkv), last), place, True)
    cols = width // 2
    own_cols = lax.dynamic_slice_in_dim(flat(d_proj), low * cols, cols, 1)
    attended = jnp.concatenate(by_core(flat(att), flat(att_other)), axis=1)
    out_mine, out_other = weight_grad(after(attended, qkv_mine), own_cols, place, True)
    attn_mine = jnp.concatenate([qkv_mine, out_mine], axis=2)
    attn_there = y_swap(jnp.concatenate([qkv_other, out_other], axis=2))
    d_h, sums_in = inputs_back(after(part_two, attn_mine), two_there, h, d_mid, mods, F32)
    last = begin("up", y_add(up_mine, after(up_there, d_h)))
    last = step("down", 3, last)
    last = step("up", 2, last)

    d_gate_two = jnp.sum(g.astype(F32) * mlp_out, axis=1)
    d_mod = jnp.concatenate([part.reshape(latents, -1) for part in (sums_in, sums_mid, d_gate_two)], axis=1)
    d_mine = after(d_mod.astype(BF), last)
    d_there = y_swap(d_mine)
    last = begin("attn", y_add(attn_mine, after(attn_there, d_mine)))
    last = down_part = step("down", 4 if ring else n_fsdp, last)
    down_there = y_swap(down_part)
    last = step("up", 3, last)
    d_there = after(d_there, last)
    d_six = jnp.where(
        high == 0, jnp.concatenate([d_mine, d_there]), jnp.concatenate([d_there, d_mine])
    )
    d_all = gather_back(after(d_six, last), "fsdp")
    last = step("attn", 2, last)
    last = up_part = step("up", 4 if ring else n_fsdp, last)
    up_last, up_core = y_swap(up_part), core_swap(up_part)
    d_all = together(d_all, last).reshape(-1, d_six.shape[1])
    d_silu = mm_nt(d_all, ada).reshape(n_fsdp, 2 * latents, share)
    d_silu = send_back(d_silu, "fsdp")
    last = step("attn", 3, last)
    ada_cols = ada.shape[1] // n_seq
    g_ada = mm_tn(silu_cols, lax.dynamic_slice_in_dim(after(d_all, last), seq * ada_cols, ada_cols, 1))
    last = attn_part = step("attn", 4 if ring else n_fsdp, last)
    attn_last, attn_core = y_swap(attn_part), core_swap(attn_part)

    d_silu = together(d_silu, last)
    ordered = jnp.concatenate([d_silu, d_silu[:-1]])
    d_silu = lax.dynamic_slice_in_dim(ordered, (n_fsdp - fsdp) % n_fsdp, n_fsdp, 0)
    d_silu = d_silu.transpose(1, 0, 2).reshape(2 * latents, width)
    cond_grad = jax.vjp(jax.nn.silu, cond)[1](d_silu)[0]

    down_sum = y_add(down_part, down_there)
    g_down = jnp.concatenate(by_core(down_sum, core_swap(down_sum))).astype(F32)
    g_up = finish((up_part, up_last, up_core, core_swap(up_last)), (n_fsdp,), place)[0]
    g_qkv, g_out = finish((attn_part, attn_last, attn_core, core_swap(attn_last)), (3, 1), place)

    result = jnp.where(on_first, d_h, layer_out)
    blocks = result.reshape(latents, 2, 2, tokens_here, width)
    blocks = lax.dynamic_index_in_dim(blocks, low, 1, keepdims=False)
    keep = blocks[:, 0]
    arrive = after(y_swap(blocks[:, 1].astype(BF)), attn_part).astype(F32)
    end_rows = jnp.where(
        high == 0, jnp.concatenate([keep, arrive], axis=0), jnp.concatenate([arrive, keep], axis=0)
    )
    return (
        end_rows[None],
        cond_grad[None],
        g_ada[None],
        g_qkv[None],
        g_out[None],
        g_up[None],
        g_down[None],
    )


def solution(mesh):
    rows = P("section", "fsdp", "seq", None)
    weight = P("section", "fsdp", None)
    return jax.shard_map(
        body,
        mesh=mesh,
        in_specs=(rows, P("fsdp"), P("fsdp"), P(), weight, weight, weight, weight, weight),
        out_specs=(rows, weight, P("section", "fsdp", "seq"), weight, weight, weight, weight),
        check_vma=False,
    )
```
